256 devices in a mesh: comp: 16 (over z, core), pts: 16 (over x, y).
Axes of the slice: x: 4, y: 4, z: 8, core: 2. Of those that a mesh axis runs over, the one named last changes fastest.
Arguments:
- spectra: bfloat16 [3600, 18432], P('comp', 'pts'), may hold values from 0.049804688 to 2
- land_mask: int32 [128, 3600], P('pts'), may hold values from 0 to 1, as said below
- send_rows: int32 [16, 16, 1280], P('pts'), may hold values from 0 to 28799, as said below
- row_counts: int32 [16, 16], replicated, may hold values from 360 to 1280, as said below
- return_index: int32 [16, 13120], P('pts'), may hold values from 0 to 13119, as said below
Outputs:
- owned: bfloat16 [144, 209920], P('comp', 'pts')
The draws below stay inside these ranges and needn't reach their ends.
Inputs may be any that keep to these rules, and one draw needn't show every extreme that they name: land_mask is 1 exactly at the cells named by the first row_counts[j, d] entries of send_rows[j, d], over all j and d. For k < row_counts[j, d], send_rows[j, d, k] names a cell of band j; all named cells are distinct; entries past the count are 0. For every owner d the sum over j of row_counts[j, d] is 13120. `return_index`: each row is a permutation of 0 to 13119.
All inputs are finite; a program needn't handle non-finite values.
Results may differ from the reference program's by a relative error of at most 0.001.
Values may be sent and summed in bfloat16 or wider, within the bound.
A program may use at most 64 MiB of HBM per device.

```python
import math
import jax
import jax.numpy as jnp
from jax import lax

ND = 36
NF = 4
ITERS = 4
LON = 3600
LAT_DEV = 8
COMP = 144
LAT = 128
CAP = 1280
SEA_DEV = 13120
N_PTS = 16


def route_plan(key):
    level_step = CAP // (2 * N_PTS)
    eighth = CAP // 8
    cell_count = LAT_DEV * LON
    band_levels = level_step * jax.random.permutation(jax.random.fold_in(key, 11), N_PTS)
    sign_pattern = jax.random.permutation(jax.random.fold_in(key, 12), 2 * (jnp.arange(N_PTS, dtype=jnp.int32) % 2) - 1)
    base_count = CAP - level_step * (N_PTS - 1) - eighth
    src_ids = jnp.arange(N_PTS, dtype=jnp.int32)[:, None]
    dst_ids = jnp.arange(N_PTS, dtype=jnp.int32)[None, :]
    counts_all = (band_levels[:, None] + eighth * sign_pattern[(dst_ids - src_ids) % N_PTS] + base_count).astype(jnp.int32)
    band_keys = jax.random.split(jax.random.fold_in(key, 13), N_PTS)
    cell_order = jax.vmap(lambda band_key: jax.random.permutation(band_key, cell_count))(band_keys).astype(jnp.int32)
    offsets = jnp.cumsum(counts_all, axis=1) - counts_all
    slot_ids = jnp.arange(CAP, dtype=jnp.int32)
    positions = jnp.minimum(offsets[:, :, None] + slot_ids[None, None, :], cell_count - 1)
    chosen = jnp.take_along_axis(cell_order, positions.reshape(N_PTS, -1), axis=1).reshape(N_PTS, N_PTS, CAP)
    sends = jnp.where(slot_ids[None, None, :] < counts_all[:, :, None], chosen, 0).astype(jnp.int32)
    totals = jnp.sum(counts_all, axis=1)
    listed = (jnp.arange(cell_count, dtype=jnp.int32)[None, :] < totals[:, None]).astype(jnp.int32)
    band_mask = jnp.zeros((N_PTS, cell_count), jnp.int32).at[jnp.arange(N_PTS)[:, None], cell_order].set(listed)
    return (band_mask.reshape(N_PTS * LAT_DEV, LON), sends, counts_all)


def draw_land_mask(key, part):
    return route_plan(key)[0]


def draw_send_rows(key, part):
    return route_plan(key)[1]


def draw_row_counts(key, part):
    return route_plan(key)[2]


def draw_return_index(key, part):
    owner_keys = jax.random.split(jax.random.fold_in(key, 21), N_PTS)
    return jax.vmap(lambda owner_key: jax.random.permutation(owner_key, SEA_DEV))(owner_keys).astype(jnp.int32)


def level_of(rng, dims, cuts, low, high):
    def one(position, blocks):
        steps = jax.random.uniform(jax.random.fold_in(jax.random.fold_in(rng, 6), position), (blocks,), jnp.float32, low / len(cuts), high / len(cuts))
        return jnp.repeat(jnp.exp(steps), dims[position] // blocks).reshape((-1,) + (1,) * (len(dims) - position - 1))

    level = one(*cuts[0])
    for cut in cuts[1:]:
        level = level * one(*cut)
    return level


def setup_inputs(seed: int = 0) -> dict:
    seeds = jax.random.split(jax.random.key(seed), 6)
    return {
        "spectra": jnp.clip(jnp.exp(math.log(2.0) - 3.6927934 * jax.random.uniform(seeds[0], (LON, LAT * COMP), jnp.float32) ** level_of(seeds[0], (LON, LAT * COMP), ((0, 16), (1, 16)), -0.2, 0.2)), 0.049804688, 2.0).astype(jnp.bfloat16),
        "land_mask": draw_land_mask(jax.random.fold_in(seeds[5], 71), 0),
        "send_rows": draw_send_rows(jax.random.fold_in(seeds[5], 71), 0),
        "row_counts": draw_row_counts(jax.random.fold_in(seeds[5], 71), 0),
        "return_index": draw_return_index(jax.random.fold_in(seeds[5], 71), 0),
    }


def lon_parts(values, periodic):
    if periodic:
        return jnp.roll(values, 1, axis=-1), values, jnp.roll(values, -1, axis=-1)
    return values[..., :-2], values[..., 1:-1], values[..., 2:]


def latitude_cosines(first_row, row_total, grid_rows):
    row_ids = (first_row + jnp.arange(row_total)).astype(jnp.float32)
    degrees = 45.0 + 0.1 * (row_ids + 0.5 - 0.5 * grid_rows)
    radians = degrees * (math.pi / 180.0)
    return jnp.cos(radians), jnp.cos(radians + 0.05 * math.pi / 180.0)


def courant_pairs(comp_ids, grid_rows):
    freq_ids = (comp_ids // ND).astype(jnp.float32)
    dir_ids = (comp_ids % ND).astype(jnp.float32)
    angles = (dir_ids + 0.5) * (2.0 * math.pi / ND)
    top_cos = math.cos((45.0 + 0.05 * grid_rows) * math.pi / 180.0)
    speed_ratio = 0.6 * top_cos * jnp.power(jnp.float32(1.1), -freq_ids)
    return speed_ratio * jnp.cos(angles), speed_ratio * jnp.sin(angles)


def advance(values, sea_mask, cos_mid, cos_north, east_x, north_y, periodic):
    western, centre, eastern = lon_parts(values[:, 1:-1], periodic)
    northern = lon_parts(values[:, 2:], periodic)[1]
    southern = lon_parts(values[:, :-2], periodic)[1]
    mask_west, mask_centre, mask_east = lon_parts(sea_mask[1:-1], periodic)
    mask_north = lon_parts(sea_mask[2:], periodic)[1]
    mask_south = lon_parts(sea_mask[:-2], periodic)[1]
    inner_cos = cos_mid[1:-1][None, :, None]
    courant_x = east_x[:, None, None] / inner_cos
    ahead_x = jnp.maximum(courant_x, 0.0)
    behind = jnp.minimum(courant_x, 0.0)
    flux_east = (ahead_x * centre + behind * eastern) * (mask_centre * mask_east)
    flux_west = (ahead_x * western + behind * centre) * (mask_west * mask_centre)
    across = north_y[:, None, None]
    upward = jnp.maximum(across, 0.0)
    downward = jnp.minimum(across, 0.0)
    flux_north = (upward * centre + downward * northern) * (mask_centre * mask_north) * cos_north[1:-1][None, :, None]
    flux_south = (upward * southern + downward * centre) * (mask_south * mask_centre) * cos_north[:-2][None, :, None]
    updated = mask_centre * (centre - (flux_east - flux_west) - (flux_north - flux_south) / inner_cos)
    return updated, mask_centre


def reference(spectra, land_mask, send_rows, row_counts, return_index):
    grid_rows = LAT_DEV * N_PTS
    padded_mask = jnp.pad(land_mask.astype(jnp.float32), ((1, 1), (0, 0)))
    cos_mid, cos_north = latitude_cosines(-1, grid_rows + 2, grid_rows)

    def propagate(inputs):
        spec_block, comp_ids = inputs
        east_x, north_y = courant_pairs(comp_ids, grid_rows)
        values = spec_block.astype(jnp.float32)
        for _ in range(ITERS):
            values, kept_mask = advance(jnp.pad(values, ((0, 0), (1, 1), (0, 0))), padded_mask, cos_mid, cos_north, east_x, north_y, True)
        return values.astype(jnp.bfloat16)

    grid_view = jnp.transpose(spectra.reshape(LON, grid_rows, COMP), (2, 1, 0))
    spec_blocks = grid_view.reshape(NF, ND, grid_rows, LON)
    comp_table = jnp.arange(COMP, dtype=jnp.int32).reshape(NF, ND)
    propagated = lax.map(propagate, (spec_blocks, comp_table)).reshape(COMP, grid_rows * LON)

    def owner_cells(owner_id, picked):
        counts_in = row_counts[:, owner_id]
        offsets = (jnp.cumsum(counts_in) - counts_in).astype(jnp.int32)
        source = (jnp.sum((picked[:, None] >= offsets[None, :]).astype(jnp.int32), axis=1) - 1).astype(jnp.int32)
        within = (picked - offsets[source]).astype(jnp.int32)
        local_cell = send_rows[source, owner_id, within]
        return (local_cell + source * (LAT_DEV * LON)).astype(jnp.int32)

    cell_ids = jax.vmap(owner_cells)(jnp.arange(N_PTS, dtype=jnp.int32), return_index)
    return jnp.take(propagated, cell_ids.reshape(-1), axis=1)
```

```python
import functools
import math

import jax
import jax.numpy as jnp
from jax import lax
from jax.experimental import pallas as pl
from jax.experimental.pallas import tpu as pltpu
from jax.sharding import PartitionSpec as P

ND = 36
ITERS = 4
LANES = 128
CB = 9
ROWS = 8
OWN = ITERS * CB
LON = 3600
LB = 225
SEG = 80
NB = 16
PAD = 8
GROUPS = 14
CAP = 1280
CAP_ROWS = 96
SLOT_ROWS = 1024
SLOT_GROUPS = 13
F32 = jnp.float32
BF16 = jnp.bfloat16


def iota(shape, dim):
    return lax.broadcasted_iota(jnp.int32, shape, dim)


def one_hot(cond):
    return jnp.where(cond, 1.0, 0.0).astype(BF16)


def mm(a, b):
    return jnp.dot(a, b, preferred_element_type=F32)


def propagate_kernel(
    x_ref, mask_ref, coef_ref, out_ref,
    sendbuf, piece, hsend, hrecv, ymid, mprev, mnext, mstack, mexp, mdown, kbuf, va, vb,
    s_send, s_recv, h_send, h_recv, m_send, m_recv, l_sem,
):
    c = lax.axis_index("comp")
    j = lax.axis_index("pts")
    nxt = lax.rem(j + 1, NB)
    prv = lax.rem(j + NB - 1, NB)
    quad = lax.rem(c, 4)
    north = quad < 2
    east = jnp.logical_or(quad == 0, quad == 3)
    down = jnp.where(north, nxt, prv)

    barrier = pltpu.get_barrier_semaphore()
    for s in range(1, NB):
        pl.semaphore_signal(
            barrier, inc=1, device_id={"comp": lax.rem(c + s, NB)}, device_id_type=pl.DeviceIdType.MESH
        )
    for other in (nxt, prv):
        pl.semaphore_signal(barrier, inc=1, device_id={"pts": other}, device_id_type=pl.DeviceIdType.MESH)

    ymid[LB : 3 * SEG, :] = jnp.zeros((3 * SEG - LB, LANES), F32)
    m_id = iota((ROWS * NB * CB, LANES), 0)
    lane = iota((1, LANES), 1)
    pos = lane // CB
    lane_s = iota((SEG, LANES), 1)
    x = x_ref[...]
    for t in range(NB):
        row = pos if t % 4 < 2 else ROWS - 1 - pos
        want = jnp.where(lane < ROWS * CB, row * (NB * CB) + t * CB + lane - pos * CB, -1)
        ymid[0:LB, :] = mm(x, one_hot(m_id == want))
        y0 = ymid[0:SEG, :]
        y1 = pltpu.roll(ymid[SEG : 2 * SEG, :], 72, 1)
        y2 = pltpu.roll(ymid[2 * SEG : 3 * SEG, :], 16, 1)
        sendbuf[t, :, 0:LANES] = jnp.where(lane_s < 72, y0, y1).astype(BF16)
        sendbuf[t, :, LANES : 2 * LANES] = jnp.where(lane_s < 16, y1, y2).astype(BF16)

    pl.semaphore_wait(barrier, NB + 1)

    copies = []
    for s in range(1, NB):
        to = lax.rem(c + s, NB)
        copies.append(
            pltpu.make_async_remote_copy(
                src_ref=sendbuf.at[to], dst_ref=piece.at[c], send_sem=s_send.at[to], recv_sem=s_recv.at[c],
                device_id={"comp": to}, device_id_type=pl.DeviceIdType.MESH,
            )
        )
        copies[-1].start()
    m_up = pltpu.make_async_remote_copy(
        src_ref=mask_ref, dst_ref=mprev, send_sem=m_send.at[0], recv_sem=m_recv.at[0],
        device_id={"pts": nxt}, device_id_type=pl.DeviceIdType.MESH,
    )
    m_up.start()
    m_dn = pltpu.make_async_remote_copy(
        src_ref=mask_ref, dst_ref=mnext, send_sem=m_send.at[1], recv_sem=m_recv.at[1],
        device_id={"pts": prv}, device_id_type=pl.DeviceIdType.MESH,
    )
    m_dn.start()
    own = pltpu.make_async_copy(sendbuf.at[c], piece.at[c], l_sem)
    own.start()

    m_up.wait()
    m_dn.wait()
    mstack[0:ROWS, :] = jnp.where(j > 0, mprev[...], 0).astype(F32)
    mstack[ROWS : 2 * ROWS, :] = mask_ref[...].astype(F32)
    mstack[2 * ROWS : 3 * ROWS, :] = jnp.where(j < NB - 1, mnext[...], 0).astype(F32)
    g_id = iota((3 * ROWS, LANES), 0)
    l_id = iota((3 * ROWS, LANES), 1)
    rr = l_id // CB
    live = rr < ROWS + ITERS
    e_here = one_hot(jnp.logical_and(live, g_id == jnp.where(north, rr + 4, 19 - rr)))
    e_down = one_hot(jnp.logical_and(live, g_id == jnp.where(north, rr + 5, 18 - rr)))
    e_both = jnp.concatenate([e_here, e_down], axis=1)
    stack = mstack[...].astype(BF16)
    both = lax.dot_general(stack, e_both, (((0,), (0,)), ((), ())), preferred_element_type=F32)
    mexp[PAD : PAD + LON, :] = both[:, :LANES]
    mdown[...] = both[:, LANES:]
    mexp[PAD - 1 : PAD, :] = mexp[PAD + LON - 1 : PAD + LON, :]
    mexp[PAD + LON : PAD + LON + 1, :] = mexp[PAD : PAD + 1, :]
    ax = coef_ref[0:1, :]
    ay = coef_ref[1:2, :]
    ad = coef_ref[2:3, :]
    step_rows = 120
    for i in range(LON // step_rows):
        a = PAD + i * step_rows
        m = mexp[a : a + step_rows, :]
        lon_down = jnp.where(
            east, mexp[a + 1 : a + 1 + step_rows, :], mexp[a - 1 : a - 1 + step_rows, :]
        )
        kbuf[i * step_rows : (i + 1) * step_rows, :] = m * (
            1.0 - ax * lon_down - ad * mdown[i * step_rows : (i + 1) * step_rows, :]
        )

    src = iota((2 * LANES, LANES), 0)
    dst = iota((2 * LANES, LANES), 1)
    seg = dst // OWN
    h_pack = one_hot(
        jnp.logical_and(seg < 3, src == seg * (ROWS * CB) + (ROWS - ITERS) * CB + dst - seg * OWN)
    )
    hops = []
    for b in range(NB):

        @pl.when(b == c)
        def _():
            own.wait()

        @pl.when(b != c)
        def _():
            pltpu.make_async_remote_copy(
                src_ref=sendbuf.at[b], dst_ref=piece.at[b], send_sem=s_send.at[b], recv_sem=s_recv.at[b],
                device_id={"comp": b}, device_id_type=pl.DeviceIdType.MESH,
            ).wait_recv()

        hsend[b] = mm(piece[b], h_pack).astype(BF16)
        hops.append(
            pltpu.make_async_remote_copy(
                src_ref=hsend.at[b], dst_ref=hrecv.at[b], send_sem=h_send.at[b], recv_sem=h_recv.at[b],
                device_id={"pts": down}, device_id_type=pl.DeviceIdType.MESH,
            )
        )
        hops[-1].start()

    u_src = iota((2 * LANES, 3 * LANES), 0)
    u_dst = iota((2 * LANES, 3 * LANES), 1)
    u_seg = u_dst // LANES
    u_lane = u_dst - u_seg * LANES
    own_lane = jnp.logical_and(u_lane >= OWN, u_lane < OWN + ROWS * CB)
    unpack = one_hot(jnp.logical_and(own_lane, u_src == u_seg * (ROWS * CB) + u_lane - OWN))
    hu_src = iota((LANES, 3 * LANES), 0)
    hu_dst = iota((LANES, 3 * LANES), 1)
    hu_seg = hu_dst // LANES
    hu_lane = hu_dst - hu_seg * LANES
    h_unpack = one_hot(jnp.logical_and(hu_lane < OWN, hu_src == hu_seg * OWN + hu_lane))
    for b in range(NB):
        hops[b].wait_recv()
        full = mm(piece[b], unpack) + mm(hrecv[b], h_unpack)
        for t in range(3):
            size = min(SEG, LB - t * SEG)
            a = PAD + b * LB + t * SEG
            va[a : a + size, :] = full[:size, t * LANES : (t + 1) * LANES] * mexp[a : a + size, :]

    for it in range(ITERS):
        v, w = (va, vb) if it % 2 == 0 else (vb, va)
        v[PAD - 1 : PAD, :] = v[PAD + LON - 1 : PAD + LON, :]
        v[PAD + LON : PAD + LON + 1, :] = v[PAD : PAD + 1, :]
        for i in range(LON // step_rows):
            a = PAD + i * step_rows
            k = i * step_rows
            here = v[a : a + step_rows, :]
            side = jnp.where(east, v[a - 1 : a - 1 + step_rows, :], v[a + 1 : a + 1 + step_rows, :])
            new = kbuf[k : k + step_rows, :] * here + mexp[a : a + step_rows, :] * (
                ax * side + ay * pltpu.roll(here, CB, 1)
            )
            if it < ITERS - 1:
                w[a : a + step_rows, :] = new
            else:
                out_ref[k : k + step_rows, :] = new.astype(BF16)

    for copy in copies:
        copy.wait_send()
    for hop in hops:
        hop.wait_send()


def propagate(x, mask, coef):
    dma = pltpu.SemaphoreType.DMA
    vmem = pl.BlockSpec(memory_space=pltpu.VMEM)
    wrapped = PAD + LON + 8
    return pl.pallas_call(
        propagate_kernel,
        out_shape=jax.ShapeDtypeStruct((LON, LANES), BF16),
        in_specs=[vmem, vmem, vmem],
        out_specs=vmem,
        scratch_shapes=[
            pltpu.VMEM((NB, SEG, 2 * LANES), BF16),
            pltpu.VMEM((NB, SEG, 2 * LANES), BF16),
            pltpu.VMEM((NB, SEG, LANES), BF16),
            pltpu.VMEM((NB, SEG, LANES), BF16),
            pltpu.VMEM((3 * SEG, LANES), F32),
            pltpu.VMEM((ROWS, LON), jnp.int32),
            pltpu.VMEM((ROWS, LON), jnp.int32),
            pltpu.VMEM((3 * ROWS, LON), F32),
            pltpu.VMEM((wrapped, LANES), F32),
            pltpu.VMEM((LON, LANES), F32),
            pltpu.VMEM((LON, LANES), F32),
            pltpu.VMEM((wrapped, LANES), F32),
            pltpu.VMEM((wrapped, LANES), F32),
            dma((NB,)), dma((NB,)), dma((NB,)), dma((NB,)), dma((2,)), dma((2,)), dma,
        ],
        compiler_params=pltpu.CompilerParams(
            collective_id=0, has_side_effects=True, vmem_limit_bytes=40 << 20
        ),
        name="propagate",
    )(x, mask, coef)


def select_kernel(rows_ref, idx_ref, v_ref, out_ref, tab, stage):
    src = iota((LANES, 2 * LANES), 0)
    dst = iota((LANES, 2 * LANES), 1)
    half = dst // LANES
    lane2 = dst - half * LANES
    chunk = 240
    for pair in range(ROWS // 2):
        spread = one_hot(
            jnp.logical_and(
                lane2 < GROUPS * CB, src == OWN + (2 * pair + half) * CB + lane2 - (lane2 // CB) * CB
            )
        )

        def fill(i, _, spread=spread, pair=pair):
            a = pl.multiple_of(i * chunk, chunk)
            both = mm(v_ref[pl.ds(a, chunk), :], spread)
            tab[pl.ds(2 * pair * LON + a, chunk), :] = both[:, :LANES]
            tab[pl.ds((2 * pair + 1) * LON + a, chunk), :] = both[:, LANES:]
            return 0

        lax.fori_loop(0, LON // chunk, fill, 0)

    lane = iota((1, LANES), 1)
    unroll = 2

    def owner(d, _):
        base = d * (CAP_ROWS * GROUPS)

        def block(q, _):
            for u in range(unroll):
                r = q * unroll + u
                e = base + r * GROUPS
                acc = tab[pl.ds(idx_ref[e], 1), :]
                for g in range(1, GROUPS):
                    acc = jnp.where(lane >= CB * g, tab[pl.ds(idx_ref[e + g], 1), :], acc)
                stage[pl.ds(r, 1), :] = acc
            return 0

        lax.fori_loop(0, rows_ref[d], block, 0)
        out_ref[d] = stage[...].astype(BF16)
        return 0

    lax.fori_loop(0, NB, owner, 0)


def select_cells(rows, idx, v):
    smem = pl.BlockSpec(memory_space=pltpu.SMEM)
    vmem = pl.BlockSpec(memory_space=pltpu.VMEM)
    return pl.pallas_call(
        select_kernel,
        out_shape=jax.ShapeDtypeStruct((NB, CAP_ROWS, LANES), BF16),
        in_specs=[smem, smem, vmem],
        out_specs=vmem,
        scratch_shapes=[pltpu.VMEM((ROWS * LON, LANES), F32), pltpu.VMEM((CAP_ROWS, LANES), F32)],
        compiler_params=pltpu.CompilerParams(vmem_limit_bytes=40 << 20),
        name="select_cells",
    )(rows, idx, v)


def exchange_kernel(src_ref, out_ref, send, recv, l_sem):
    j = lax.axis_index("pts")
    barrier = pltpu.get_barrier_semaphore()
    for s in range(1, NB):
        pl.semaphore_signal(
            barrier, inc=1, device_id={"pts": lax.rem(j + s, NB)}, device_id_type=pl.DeviceIdType.MESH
        )
    own = pltpu.make_async_copy(src_ref.at[j], out_ref.at[j], l_sem)
    own.start()
    pl.semaphore_wait(barrier, NB - 1)
    copies = []
    for s in range(1, NB):
        to = lax.rem(j + s, NB)
        copies.append(
            pltpu.make_async_remote_copy(
                src_ref=src_ref.at[to], dst_ref=out_ref.at[j], send_sem=send.at[s], recv_sem=recv.at[s],
                device_id={"pts": to}, device_id_type=pl.DeviceIdType.MESH,
            )
        )
        copies[-1].start()
    own.wait()
    for copy in copies:
        copy.wait()


def exchange(outgoing):
    vmem = pl.BlockSpec(memory_space=pltpu.VMEM)
    return pl.pallas_call(
        exchange_kernel,
        out_shape=jax.ShapeDtypeStruct(outgoing.shape, outgoing.dtype),
        in_specs=[vmem],
        out_specs=vmem,
        scratch_shapes=[
            pltpu.SemaphoreType.DMA((NB,)), pltpu.SemaphoreType.DMA((NB,)), pltpu.SemaphoreType.DMA,
        ],
        compiler_params=pltpu.CompilerParams(collective_id=1, has_side_effects=True),
        name="exchange",
    )(outgoing)


def collect_kernel(idx_ref, rec_ref, out_ref, tab, stage):
    src = iota((LANES, 2 * LANES), 0)
    dst = iota((LANES, 2 * LANES), 1)
    half = dst // LANES
    lane2 = dst - half * LANES
    total = NB * CAP_ROWS
    for pair in range(GROUPS // 2):
        spread = one_hot(
            jnp.logical_and(
                lane2 < SLOT_GROUPS * CB, src == (2 * pair + half) * CB + lane2 - (lane2 // CB) * CB
            )
        )

        def fill(i, _, spread=spread, pair=pair):
            both = mm(rec_ref[i], spread)
            a = pl.multiple_of(i * CAP_ROWS, CAP_ROWS)
            tab[pl.ds(2 * pair * total + a, CAP_ROWS), :] = both[:, :LANES]
            tab[pl.ds((2 * pair + 1) * total + a, CAP_ROWS), :] = both[:, LANES:]
            return 0

        lax.fori_loop(0, NB, fill, 0)

    lane = iota((1, LANES), 1)
    unroll = 8

    def block(q, _):
        for u in range(unroll):
            r = q * unroll + u
            acc = tab[pl.ds(idx_ref[r], 1), :]
            for g in range(1, SLOT_GROUPS):
                acc = jnp.where(lane >= CB * g, tab[pl.ds(idx_ref[g * SLOT_ROWS + r], 1), :], acc)
            stage[pl.ds(r, 1), :] = acc
        return 0

    lax.fori_loop(0, SLOT_ROWS // unroll, block, 0)
    s_row = iota((SLOT_GROUPS * 16, LANES), 0)
    s_lane = iota((SLOT_GROUPS * 16, LANES), 1)
    group = s_row // 16
    comp = s_row - group * 16
    turn = one_hot(jnp.logical_and(comp < CB, s_lane == group * CB + comp))
    width = out_ref.shape[1]
    turned = lax.dot_general(
        turn, stage[...].astype(BF16), (((1,), (1,)), ((), ())), preferred_element_type=F32
    )
    for g in range(SLOT_GROUPS):
        size = min(SLOT_ROWS, width - g * SLOT_ROWS)
        out_ref[:, g * SLOT_ROWS : g * SLOT_ROWS + size] = turned[16 * g : 16 * g + CB, :size].astype(BF16)


def collect(idx, received, width):
    smem = pl.BlockSpec(memory_space=pltpu.SMEM)
    vmem = pl.BlockSpec(memory_space=pltpu.VMEM)
    return pl.pallas_call(
        collect_kernel,
        out_shape=jax.ShapeDtypeStruct((CB, width), BF16),
        in_specs=[smem, vmem],
        out_specs=vmem,
        scratch_shapes=[
            pltpu.VMEM((GROUPS * NB * CAP_ROWS, LANES), F32), pltpu.VMEM((SLOT_ROWS, LANES), F32),
        ],
        compiler_params=pltpu.CompilerParams(vmem_limit_bytes=40 << 20),
        name="collect",
    )(idx, received)


def coefficients(comp_here, pts_here):
    grid_rows = ROWS * NB
    lane = jnp.arange(LANES, dtype=jnp.int32)
    rr = lane // CB
    comp = comp_here * CB + lane % CB
    quad = comp_here % 4
    north = quad < 2
    band_row = jnp.where(north, rr - ITERS, ROWS - 1 + ITERS - rr)
    row = (pts_here * ROWS + band_row).astype(F32)

    def cosines(row_ids):
        radians = (45.0 + 0.1 * (row_ids + 0.5 - 0.5 * grid_rows)) * (math.pi / 180.0)
        return jnp.cos(radians), jnp.cos(radians + 0.05 * math.pi / 180.0)

    cos_mid, cos_upper = cosines(row)
    cos_lower = cosines(row - 1.0)[1]
    freq = (comp // ND).astype(F32)
    angle = ((comp % ND).astype(F32) + 0.5) * (2.0 * math.pi / ND)
    top = math.cos((45.0 + 0.05 * grid_rows) * math.pi / 180.0)
    speed = 0.6 * top * jnp.power(jnp.float32(1.1), -freq)
    east_x = jnp.abs(speed * jnp.cos(angle))
    north_y = jnp.abs(speed * jnp.sin(angle))
    ax = east_x / cos_mid
    up = north_y * jnp.where(north, cos_lower, cos_upper) / cos_mid
    dn = north_y * jnp.where(north, cos_upper, cos_lower) / cos_mid
    live = rr < ROWS + ITERS
    rows = [jnp.where(live, value, 0.0) for value in (ax, up, dn)]
    return jnp.stack(rows + [jnp.zeros((LANES,), F32)] * 5)


def local(spectra, land_mask, send_rows, row_counts, return_index):
    comp_here = lax.axis_index("comp")
    pts_here = lax.axis_index("pts")
    north = comp_here % 4 < 2

    cells = send_rows[0]
    row = cells // LON
    cell_row = jnp.where(north, row, ROWS - 1 - row) * LON + cells - row * LON
    cell_idx = jnp.pad(cell_row, ((0, 0), (0, CAP_ROWS * GROUPS - CAP))).reshape(-1)
    counts_out = lax.dynamic_slice_in_dim(row_counts, pts_here, 1, 0)[0]
    blocks = (counts_out + 2 * GROUPS - 1) // (2 * GROUPS)

    counts_in = lax.dynamic_slice_in_dim(row_counts, pts_here, 1, 1)[:, 0]
    offsets = jnp.cumsum(counts_in) - counts_in
    picked = return_index[0]
    source = jnp.sum((picked[:, None] >= offsets[None, :]).astype(jnp.int32), axis=1) - 1
    start = jnp.sum(
        jnp.where(source[:, None] == jnp.arange(NB, dtype=jnp.int32)[None, :], offsets[None, :], 0), axis=1
    )
    within = picked - start
    slot_row = within // GROUPS
    slot = (within - slot_row * GROUPS) * (NB * CAP_ROWS) + source * CAP_ROWS + slot_row
    slot_idx = jnp.pad(slot, (0, SLOT_ROWS * SLOT_GROUPS - slot.shape[0]))

    values = propagate(spectra, land_mask, coefficients(comp_here, pts_here))
    outgoing = select_cells(blocks, cell_idx, values)
    received = exchange(outgoing)
    return collect(slot_idx, received, picked.shape[0])


def solution(mesh):
    placed = (P("comp", "pts"), P("pts", None), P("pts", None, None), P(), P("pts", None))
    return jax.shard_map(
        local, mesh=mesh, in_specs=placed, out_specs=P("comp", "pts"), check_vma=False
    )
```

```python
import functools
import math

import jax
import jax.numpy as jnp
from jax import lax
from jax.experimental import pallas as pl
from jax.experimental.pallas import tpu as pltpu
from jax.sharding import PartitionSpec as P

ND = 36
ITERS = 4
LANES = 128
CB = 9
ROWS = 8
OWN = ITERS * CB
LON = 3600
LB = 225
SEG = 80
NB = 16
PAD = 8
GROUPS = 14
CAP = 1280
CAP_ROWS = 96
SLOT_ROWS = 1024
SLOT_GROUPS = 13
F32 = jnp.float32
BF16 = jnp.bfloat16


def iota(shape, dim):
    return lax.broadcasted_iota(jnp.int32, shape, dim)


def one_hot(cond):
    return jnp.where(cond, 1.0, 0.0).astype(BF16)


def mm(a, b):
    return jnp.dot(a, b, preferred_element_type=F32)


def propagate_kernel(
    x_ref, mask_ref, coef_ref, out_ref,
    sendbuf, piece, hsend, hrecv, ymid, mprev, mnext, mstack, mexp, mdown, kbuf, va, vb,
    s_send, s_recv, h_send, h_recv, m_send, m_recv, l_sem,
):
    c = lax.axis_index("comp")
    j = lax.axis_index("pts")
    nxt = lax.rem(j + 1, NB)
    prv = lax.rem(j + NB - 1, NB)
    quad = lax.rem(c, 4)
    north = quad < 2
    east = jnp.logical_or(quad == 0, quad == 3)
    down = jnp.where(north, nxt, prv)

    barrier = pltpu.get_barrier_semaphore()
    for s in range(1, NB):
        pl.semaphore_signal(
            barrier, inc=1, device_id={"comp": lax.rem(c + s, NB)}, device_id_type=pl.DeviceIdType.MESH
        )
    for other in (nxt, prv):
        pl.semaphore_signal(barrier, inc=1, device_id={"pts": other}, device_id_type=pl.DeviceIdType.MESH)

    ymid[LB : 3 * SEG, :] = jnp.zeros((3 * SEG - LB, LANES), F32)
    m_id = iota((ROWS * NB * CB, LANES), 0)
    lane = iota((1, LANES), 1)
    pos = lane // CB
    lane_s = iota((SEG, LANES), 1)
    x = x_ref[...]
    for t in range(NB):
        row = pos if t % 4 < 2 else ROWS - 1 - pos
        want = jnp.where(lane < ROWS * CB, row * (NB * CB) + t * CB + lane - pos * CB, -1)
        ymid[0:LB, :] = mm(x, one_hot(m_id == want))
        y0 = ymid[0:SEG, :]
        y1 = pltpu.roll(ymid[SEG : 2 * SEG, :], 72, 1)
        y2 = pltpu.roll(ymid[2 * SEG : 3 * SEG, :], 16, 1)
        sendbuf[t, :, 0:LANES] = jnp.where(lane_s < 72, y0, y1).astype(BF16)
        sendbuf[t, :, LANES : 2 * LANES] = jnp.where(lane_s < 16, y1, y2).astype(BF16)

    pl.semaphore_wait(barrier, NB + 1)

    copies = []
    for s in range(1, NB):
        to = lax.rem(c + s, NB)
        copies.append(
            pltpu.make_async_remote_copy(
                src_ref=sendbuf.at[to], dst_ref=piece.at[c], send_sem=s_send.at[to], recv_sem=s_recv.at[c],
                device_id={"comp": to}, device_id_type=pl.DeviceIdType.MESH,
            )
        )
        copies[-1].start()
    m_up = pltpu.make_async_remote_copy(
        src_ref=mask_ref, dst_ref=mprev, send_sem=m_send.at[0], recv_sem=m_recv.at[0],
        device_id={"pts": nxt}, device_id_type=pl.DeviceIdType.MESH,
    )
    m_up.start()
    m_dn = pltpu.make_async_remote_copy(
        src_ref=mask_ref, dst_ref=mnext, send_sem=m_send.at[1], recv_sem=m_recv.at[1],
        device_id={"pts": prv}, device_id_type=pl.DeviceIdType.MESH,
    )
    m_dn.start()
    own = pltpu.make_async_copy(sendbuf.at[c], piece.at[c], l_sem)
    own.start()

    m_up.wait()
    m_dn.wait()
    mstack[0:ROWS, :] = jnp.where(j > 0, mprev[...], 0).astype(F32)
    mstack[ROWS : 2 * ROWS, :] = mask_ref[...].astype(F32)
    mstack[2 * ROWS : 3 * ROWS, :] = jnp.where(j < NB - 1, mnext[...], 0).astype(F32)
    g_id = iota((3 * ROWS, LANES), 0)
    l_id = iota((3 * ROWS, LANES), 1)
    rr = l_id // CB
    live = rr < ROWS + ITERS
    e_here = one_hot(jnp.logical_and(live, g_id == jnp.where(north, rr + 4, 19 - rr)))
    e_down = one_hot(jnp.logical_and(live, g_id == jnp.where(north, rr + 5, 18 - rr)))
    e_both = jnp.concatenate([e_here, e_down], axis=1)
    stack = mstack[...].astype(BF16)
    both = lax.dot_general(stack, e_both, (((0,), (0,)), ((), ())), preferred_element_type=F32)
    mexp[PAD : PAD + LON, :] = both[:, :LANES]
    mdown[...] = both[:, LANES:]
    mexp[PAD - 1 : PAD, :] = mexp[PAD + LON - 1 : PAD + LON, :]
    mexp[PAD + LON : PAD + LON + 1, :] = mexp[PAD : PAD + 1, :]
    ax = coef_ref[0:1, :]
    ay = coef_ref[1:2, :]
    ad = coef_ref[2:3, :]
    step_rows = 120
    for i in range(LON // step_rows):
        a = PAD + i * step_rows
        m = mexp[a : a + step_rows, :]
        lon_down = jnp.where(
            east, mexp[a + 1 : a + 1 + step_rows, :], mexp[a - 1 : a - 1 + step_rows, :]
        )
        kbuf[i * step_rows : (i + 1) * step_rows, :] = m * (
            1.0 - ax * lon_down - ad * mdown[i * step_rows : (i + 1) * step_rows, :]
        )

    src = iota((2 * LANES, LANES), 0)
    dst = iota((2 * LANES, LANES), 1)
    seg = dst // OWN
    h_pack = one_hot(
        jnp.logical_and(seg < 3, src == seg * (ROWS * CB) + (ROWS - ITERS) * CB + dst - seg * OWN)
    )
    hops = []
    for b in range(NB):

        @pl.when(b == c)
        def _():
            own.wait()

        @pl.when(b != c)
        def _():
            pltpu.make_async_remote_copy(
                src_ref=sendbuf.at[b], dst_ref=piece.at[b], send_sem=s_send.at[b], recv_sem=s_recv.at[b],
                device_id={"comp": b}, device_id_type=pl.DeviceIdType.MESH,
            ).wait_recv()

        hsend[b] = mm(piece[b], h_pack).astype(BF16)
        hops.append(
            pltpu.make_async_remote_copy(
                src_ref=hsend.at[b], dst_ref=hrecv.at[b], send_sem=h_send.at[b], recv_sem=h_recv.at[b],
                device_id={"pts": down}, device_id_type=pl.DeviceIdType.MESH,
            )
        )
        hops[-1].start()

    u_src = iota((2 * LANES, 3 * LANES), 0)
    u_dst = iota((2 * LANES, 3 * LANES), 1)
    u_seg = u_dst // LANES
    u_lane = u_dst - u_seg * LANES
    own_lane = jnp.logical_and(u_lane >= OWN, u_lane < OWN + ROWS * CB)
    unpack = one_hot(jnp.logical_and(own_lane, u_src == u_seg * (ROWS * CB) + u_lane - OWN))
    hu_src = iota((LANES, 3 * LANES), 0)
    hu_dst = iota((LANES, 3 * LANES), 1)
    hu_seg = hu_dst // LANES
    hu_lane = hu_dst - hu_seg * LANES
    h_unpack = one_hot(jnp.logical_and(hu_lane < OWN, hu_src == hu_seg * OWN + hu_lane))
    for b in range(NB):
        hops[b].wait_recv()
        full = mm(piece[b], unpack) + mm(hrecv[b], h_unpack)
        for t in range(3):
            size = min(SEG, LB - t * SEG)
            a = PAD + b * LB + t * SEG
            va[a : a + size, :] = full[:size, t * LANES : (t + 1) * LANES] * mexp[a : a + size, :]

    for it in range(ITERS):
        v, w = (va, vb) if it % 2 == 0 else (vb, va)
        v[PAD - 1 : PAD, :] = v[PAD + LON - 1 : PAD + LON, :]
        v[PAD + LON : PAD + LON + 1, :] = v[PAD : PAD + 1, :]
        for i in range(LON // step_rows):
            a = PAD + i * step_rows
            k = i * step_rows
            here = v[a : a + step_rows, :]
            side = jnp.where(east, v[a - 1 : a - 1 + step_rows, :], v[a + 1 : a + 1 + step_rows, :])
            new = kbuf[k : k + step_rows, :] * here + mexp[a : a + step_rows, :] * (
                ax * side + ay * pltpu.roll(here, CB, 1)
            )
            if it < ITERS - 1:
                w[a : a + step_rows, :] = new
            else:
                out_ref[k : k + step_rows, :] = new.astype(BF16)

    for copy in copies:
        copy.wait_send()
    for hop in hops:
        hop.wait_send()


def propagate(x, mask, coef):
    dma = pltpu.SemaphoreType.DMA
    vmem = pl.BlockSpec(memory_space=pltpu.VMEM)
    wrapped = PAD + LON + 8
    return pl.pallas_call(
        propagate_kernel,
        out_shape=jax.ShapeDtypeStruct((LON, LANES), BF16),
        in_specs=[vmem, vmem, vmem],
        out_specs=vmem,
        scratch_shapes=[
            pltpu.VMEM((NB, SEG, 2 * LANES), BF16),
            pltpu.VMEM((NB, SEG, 2 * LANES), BF16),
            pltpu.VMEM((NB, SEG, LANES), BF16),
            pltpu.VMEM((NB, SEG, LANES), BF16),
            pltpu.VMEM((3 * SEG, LANES), F32),
            pltpu.VMEM((ROWS, LON), jnp.int32),
            pltpu.VMEM((ROWS, LON), jnp.int32),
            pltpu.VMEM((3 * ROWS, LON), F32),
            pltpu.VMEM((wrapped, LANES), F32),
            pltpu.VMEM((LON, LANES), F32),
            pltpu.VMEM((LON, LANES), F32),
            pltpu.VMEM((wrapped, LANES), F32),
            pltpu.VMEM((wrapped, LANES), F32),
            dma((NB,)), dma((NB,)), dma((NB,)), dma((NB,)), dma((2,)), dma((2,)), dma,
        ],
        compiler_params=pltpu.CompilerParams(
            collective_id=0, has_side_effects=True, vmem_limit_bytes=40 << 20
        ),
        name="propagate",
    )(x, mask, coef)


def select_kernel(rows_ref, idx_ref, v_ref, out_ref, tab, stage):
    src = iota((LANES, 2 * LANES), 0)
    dst = iota((LANES, 2 * LANES), 1)
    half = dst // LANES
    lane2 = dst - half * LANES
    for pair in range(ROWS // 2):
        spread = one_hot(
            jnp.logical_and(
                lane2 < GROUPS * CB, src == OWN + (2 * pair + half) * CB + lane2 - (lane2 // CB) * CB
            )
        )

        both = mm(v_ref[...], spread)
        tab[2 * pair * LON : (2 * pair + 1) * LON, :] = both[:, :LANES]
        tab[(2 * pair + 1) * LON : (2 * pair + 2) * LON, :] = both[:, LANES:]

    lane = iota((1, LANES), 1)
    unroll = 2

    def owner(d, _):
        base = d * (CAP_ROWS * GROUPS)

        def block(q, _):
            for u in range(unroll):
                r = q * unroll + u
                e = base + r * GROUPS
                at = idx_ref.at[pl.ds(e, GROUPS)]
                acc = tab[pl.ds(at[0], 1), :]
                for g in range(1, GROUPS):
                    acc = jnp.where(lane >= CB * g, tab[pl.ds(at[g], 1), :], acc)
                stage[pl.ds(r, 1), :] = acc
            return 0

        lax.fori_loop(0, rows_ref[d], block, 0)
        out_ref[d] = stage[...].astype(BF16)
        return 0

    lax.fori_loop(0, NB, owner, 0)


def select_cells(rows, idx, v):
    smem = pl.BlockSpec(memory_space=pltpu.SMEM)
    vmem = pl.BlockSpec(memory_space=pltpu.VMEM)
    return pl.pallas_call(
        select_kernel,
        out_shape=jax.ShapeDtypeStruct((NB, CAP_ROWS, LANES), BF16),
        in_specs=[smem, smem, vmem],
        out_specs=vmem,
        scratch_shapes=[pltpu.VMEM((ROWS * LON, LANES), F32), pltpu.VMEM((CAP_ROWS, LANES), F32)],
        compiler_params=pltpu.CompilerParams(vmem_limit_bytes=40 << 20),
        name="select_cells",
    )(rows, idx, v)


def exchange_kernel(src_ref, out_ref, send, recv, l_sem):
    j = lax.axis_index("pts")
    barrier = pltpu.get_barrier_semaphore()
    for s in range(1, NB):
        pl.semaphore_signal(
            barrier, inc=1, device_id={"pts": lax.rem(j + s, NB)}, device_id_type=pl.DeviceIdType.MESH
        )
    own = pltpu.make_async_copy(src_ref.at[j], out_ref.at[j], l_sem)
    own.start()
    pl.semaphore_wait(barrier, NB - 1)
    copies = []
    for s in range(1, NB):
        to = lax.rem(j + s, NB)
        copies.append(
            pltpu.make_async_remote_copy(
                src_ref=src_ref.at[to], dst_ref=out_ref.at[j], send_sem=send.at[s], recv_sem=recv.at[s],
                device_id={"pts": to}, device_id_type=pl.DeviceIdType.MESH,
            )
        )
        copies[-1].start()
    own.wait()
    for copy in copies:
        copy.wait()


def exchange(outgoing):
    vmem = pl.BlockSpec(memory_space=pltpu.VMEM)
    return pl.pallas_call(
        exchange_kernel,
        out_shape=jax.ShapeDtypeStruct(outgoing.shape, outgoing.dtype),
        in_specs=[vmem],
        out_specs=vmem,
        scratch_shapes=[
            pltpu.SemaphoreType.DMA((NB,)), pltpu.SemaphoreType.DMA((NB,)), pltpu.SemaphoreType.DMA,
        ],
        compiler_params=pltpu.CompilerParams(collective_id=1, has_side_effects=True),
        name="exchange",
    )(outgoing)


def collect_kernel(idx_ref, rec_ref, out_ref, tab, stage):
    src = iota((LANES, 2 * LANES), 0)
    dst = iota((LANES, 2 * LANES), 1)
    half = dst // LANES
    lane2 = dst - half * LANES
    total = NB * CAP_ROWS
    for pair in range(GROUPS // 2):
        spread = one_hot(
            jnp.logical_and(
                lane2 < SLOT_GROUPS * CB, src == (2 * pair + half) * CB + lane2 - (lane2 // CB) * CB
            )
        )

        both = mm(rec_ref[...].reshape(total, LANES), spread)
        tab[2 * pair * total : (2 * pair + 1) * total, :] = both[:, :LANES]
        tab[(2 * pair + 1) * total : (2 * pair + 2) * total, :] = both[:, LANES:]

    lane = iota((1, LANES), 1)
    unroll = 8

    def block(q, _):
        for u in range(unroll):
            r = q * unroll + u
            acc = tab[pl.ds(idx_ref[r], 1), :]
            for g in range(1, SLOT_GROUPS):
                acc = jnp.where(lane >= CB * g, tab[pl.ds(idx_ref[g * SLOT_ROWS + r], 1), :], acc)
            stage[pl.ds(r, 1), :] = acc
        return 0

    lax.fori_loop(0, SLOT_ROWS // unroll, block, 0)
    s_row = iota((SLOT_GROUPS * 16, LANES), 0)
    s_lane = iota((SLOT_GROUPS * 16, LANES), 1)
    group = s_row // 16
    comp = s_row - group * 16
    turn = one_hot(jnp.logical_and(comp < CB, s_lane == group * CB + comp))
    width = out_ref.shape[1]
    turned = lax.dot_general(
        turn, stage[...].astype(BF16), (((1,), (1,)), ((), ())), preferred_element_type=F32
    )
    for g in range(SLOT_GROUPS):
        size = min(SLOT_ROWS, width - g * SLOT_ROWS)
        out_ref[:, g * SLOT_ROWS : g * SLOT_ROWS + size] = turned[16 * g : 16 * g + CB, :size].astype(BF16)


def collect(idx, received, width):
    smem = pl.BlockSpec(memory_space=pltpu.SMEM)
    vmem = pl.BlockSpec(memory_space=pltpu.VMEM)
    return pl.pallas_call(
        collect_kernel,
        out_shape=jax.ShapeDtypeStruct((CB, width), BF16),
        in_specs=[smem, vmem],
        out_specs=vmem,
        scratch_shapes=[
            pltpu.VMEM((GROUPS * NB * CAP_ROWS, LANES), F32), pltpu.VMEM((SLOT_ROWS, LANES), F32),
        ],
        compiler_params=pltpu.CompilerParams(vmem_limit_bytes=40 << 20),
        name="collect",
    )(idx, received)


def coefficients(comp_here, pts_here):
    grid_rows = ROWS * NB
    lane = jnp.arange(LANES, dtype=jnp.int32)
    rr = lane // CB
    comp = comp_here * CB + lane % CB
    quad = comp_here % 4
    north = quad < 2
    band_row = jnp.where(north, rr - ITERS, ROWS - 1 + ITERS - rr)
    row = (pts_here * ROWS + band_row).astype(F32)

    def cosines(row_ids):
        radians = (45.0 + 0.1 * (row_ids + 0.5 - 0.5 * grid_rows)) * (math.pi / 180.0)
        return jnp.cos(radians), jnp.cos(radians + 0.05 * math.pi / 180.0)

    cos_mid, cos_upper = cosines(row)
    cos_lower = cosines(row - 1.0)[1]
    freq = (comp // ND).astype(F32)
    angle = ((comp % ND).astype(F32) + 0.5) * (2.0 * math.pi / ND)
    top = math.cos((45.0 + 0.05 * grid_rows) * math.pi / 180.0)
    speed = 0.6 * top * jnp.power(jnp.float32(1.1), -freq)
    east_x = jnp.abs(speed * jnp.cos(angle))
    north_y = jnp.abs(speed * jnp.sin(angle))
    ax = east_x / cos_mid
    up = north_y * jnp.where(north, cos_lower, cos_upper) / cos_mid
    dn = north_y * jnp.where(north, cos_upper, cos_lower) / cos_mid
    live = rr < ROWS + ITERS
    rows = [jnp.where(live, value, 0.0) for value in (ax, up, dn)]
    return jnp.stack(rows + [jnp.zeros((LANES,), F32)] * 5)


def local(spectra, land_mask, send_rows, row_counts, return_index):
    comp_here = lax.axis_index("comp")
    pts_here = lax.axis_index("pts")
    north = comp_here % 4 < 2

    cells = send_rows[0]
    row = cells // LON
    cell_row = jnp.where(north, row, ROWS - 1 - row) * LON + cells - row * LON
    cell_idx = jnp.pad(cell_row, ((0, 0), (0, CAP_ROWS * GROUPS - CAP))).reshape(-1)
    counts_out = lax.dynamic_slice_in_dim(row_counts, pts_here, 1, 0)[0]
    blocks = (counts_out + 2 * GROUPS - 1) // (2 * GROUPS)

    counts_in = lax.dynamic_slice_in_dim(row_counts, pts_here, 1, 1)[:, 0]
    offsets = jnp.cumsum(counts_in) - counts_in
    picked = return_index[0]
    source = jnp.sum((picked[:, None] >= offsets[None, :]).astype(jnp.int32), axis=1) - 1
    start = jnp.sum(
        jnp.where(source[:, None] == jnp.arange(NB, dtype=jnp.int32)[None, :], offsets[None, :], 0), axis=1
    )
    within = picked - start
    slot_row = within // GROUPS
    slot = (within - slot_row * GROUPS) * (NB * CAP_ROWS) + source * CAP_ROWS + slot_row
    slot_idx = jnp.pad(slot, (0, SLOT_ROWS * SLOT_GROUPS - slot.shape[0]))

    values = propagate(spectra, land_mask, coefficients(comp_here, pts_here))
    outgoing = select_cells(blocks, cell_idx, values)
    received = exchange(outgoing)
    return collect(slot_idx, received, picked.shape[0])


def solution(mesh):
    placed = (P("comp", "pts"), P("pts", None), P("pts", None, None), P(), P("pts", None))
    return jax.shard_map(
        local, mesh=mesh, in_specs=placed, out_specs=P("comp", "pts"), check_vma=False
    )
```

```python
import functools
import math

import jax
import jax.numpy as jnp
from jax import lax
from jax.experimental import pallas as pl
from jax.experimental.pallas import tpu as pltpu
from jax.sharding import PartitionSpec as P

ND = 36
ITERS = 4
LANES = 128
CB = 9
ROWS = 8
OWN = ITERS * CB
LON = 3600
LB = 225
SEG = 80
NB = 16
PAD = 8
GROUPS = 14
CAP = 1280
CAP_ROWS = 96
USED_ROWS = 92
SLOT_ROWS = 1024
SLOT_GROUPS = 13
F32 = jnp.float32
BF16 = jnp.bfloat16


def iota(shape, dim):
    return lax.broadcasted_iota(jnp.int32, shape, dim)


def one_hot(cond):
    return jnp.where(cond, 1.0, 0.0).astype(BF16)


def mm(a, b):
    return jnp.dot(a, b, preferred_element_type=F32)


def send(src, dst, send_sem, recv_sem, **where):
    return pltpu.make_async_remote_copy(
        src_ref=src, dst_ref=dst, send_sem=send_sem, recv_sem=recv_sem,
        device_id=where, device_id_type=pl.DeviceIdType.MESH,
    )


def merge_rows(tab, at, groups, stride, lane):
    row = tab[pl.ds(at[0], 1), :]
    for g in range(1, groups):
        row = jnp.where(lane >= CB * g, tab[pl.ds(at[g * stride], 1), :], row)
    return row


def spread_matrix(first, live):
    src = iota((LANES, 2 * LANES), 0)
    dst = iota((LANES, 2 * LANES), 1)
    half = dst // LANES
    lane2 = dst - half * LANES
    return one_hot(
        jnp.logical_and(lane2 < live * CB, src == first + half * CB + lane2 - (lane2 // CB) * CB)
    )


def partners(c):
    z = c // 2
    order = []
    for dist in (4, 3, 2, 1):
        for chip in ((4,) if dist == 4 else (dist, 8 - dist)):
            for core in range(2):
                order.append(lax.rem(z + chip, 8) * 2 + core)
    order.append(z * 2 + 1 - (c - z * 2))
    return order


def whole_kernel(
    x_ref, mask_ref, coef_ref, cell_ref, slot_ref, out_ref,
    sendbuf, piece, hsend, hrecv, ymid, mprev, mown, mnext, mstack, mexp, mdown, kbuf, va, vb,
    vfin, tab, stage, outgo, income, cells, slots,
    s_send, s_recv, h_send, h_recv, m_send, m_recv, l_sem, o_send, o_recv,
):
    c = lax.axis_index("comp")
    j = lax.axis_index("pts")
    nxt = lax.rem(j + 1, NB)
    prv = lax.rem(j + NB - 1, NB)
    quad = lax.rem(c, 4)
    north = quad < 2
    east = jnp.logical_or(quad == 0, quad == 3)
    down = jnp.where(north, nxt, prv)
    others = partners(c)

    barrier = pltpu.get_barrier_semaphore()
    for s in range(1, NB):
        pl.semaphore_signal(
            barrier, inc=1, device_id={"comp": lax.rem(c + s, NB)}, device_id_type=pl.DeviceIdType.MESH
        )
        pl.semaphore_signal(
            barrier, inc=1, device_id={"pts": lax.rem(j + s, NB)}, device_id_type=pl.DeviceIdType.MESH
        )
    get_mask = pltpu.make_async_copy(mask_ref, mown, l_sem.at[1])
    get_cells = pltpu.make_async_copy(cell_ref, cells, l_sem.at[2])
    get_slots = pltpu.make_async_copy(slot_ref, slots, l_sem.at[3])
    get_mask.start()
    get_cells.start()
    get_slots.start()

    ymid[LB : 3 * SEG, :] = jnp.zeros((3 * SEG - LB, LANES), F32)
    m_id = iota((ROWS * NB * CB, LANES), 0)
    lane = iota((1, LANES), 1)
    pos = lane // CB
    lane_s = iota((SEG, LANES), 1)
    x = x_ref[...]
    for t in range(NB):
        row = pos if t % 4 < 2 else ROWS - 1 - pos
        want = jnp.where(lane < ROWS * CB, row * (NB * CB) + t * CB + lane - pos * CB, -1)
        ymid[0:LB, :] = mm(x, one_hot(m_id == want))
        y0 = ymid[0:SEG, :]
        y1 = pltpu.roll(ymid[SEG : 2 * SEG, :], 72, 1)
        y2 = pltpu.roll(ymid[2 * SEG : 3 * SEG, :], 16, 1)
        sendbuf[t, :, 0:LANES] = jnp.where(lane_s < 72, y0, y1).astype(BF16)
        sendbuf[t, :, LANES : 2 * LANES] = jnp.where(lane_s < 16, y1, y2).astype(BF16)

    get_mask.wait()
    pl.semaphore_wait(barrier, 2 * (NB - 1))

    copies = []
    for to in others:
        copies.append(send(sendbuf.at[to], piece.at[c], s_send.at[to], s_recv.at[c], comp=to))
        copies[-1].start()
    m_up = send(mown, mprev, m_send.at[0], m_recv.at[0], pts=nxt)
    m_up.start()
    m_dn = send(mown, mnext, m_send.at[1], m_recv.at[1], pts=prv)
    m_dn.start()
    own = pltpu.make_async_copy(sendbuf.at[c], piece.at[c], l_sem.at[0])
    own.start()

    m_up.wait()
    m_dn.wait()
    mstack[0:ROWS, :] = jnp.where(j > 0, mprev[...], 0).astype(F32)
    mstack[ROWS : 2 * ROWS, :] = mown[...].astype(F32)
    mstack[2 * ROWS : 3 * ROWS, :] = jnp.where(j < NB - 1, mnext[...], 0).astype(F32)
    g_id = iota((3 * ROWS, LANES), 0)
    l_id = iota((3 * ROWS, LANES), 1)
    rr = l_id // CB
    live = rr < ROWS + ITERS
    e_here = one_hot(jnp.logical_and(live, g_id == jnp.where(north, rr + 4, 19 - rr)))
    e_down = one_hot(jnp.logical_and(live, g_id == jnp.where(north, rr + 5, 18 - rr)))
    e_both = jnp.concatenate([e_here, e_down], axis=1)
    stack = mstack[...].astype(BF16)
    both = lax.dot_general(stack, e_both, (((0,), (0,)), ((), ())), preferred_element_type=F32)
    mexp[PAD : PAD + LON, :] = both[:, :LANES]
    mdown[...] = both[:, LANES:]
    mexp[PAD - 1 : PAD, :] = mexp[PAD + LON - 1 : PAD + LON, :]
    mexp[PAD + LON : PAD + LON + 1, :] = mexp[PAD : PAD + 1, :]
    ax = coef_ref[0:1, :]
    ay = coef_ref[1:2, :]
    ad = coef_ref[2:3, :]
    step_rows = 120
    for i in range(LON // step_rows):
        a = PAD + i * step_rows
        m = mexp[a : a + step_rows, :]
        lon_down = jnp.where(
            east, mexp[a + 1 : a + 1 + step_rows, :], mexp[a - 1 : a - 1 + step_rows, :]
        )
        kbuf[i * step_rows : (i + 1) * step_rows, :] = m * (
            1.0 - ax * lon_down - ad * mdown[i * step_rows : (i + 1) * step_rows, :]
        )

    src = iota((2 * LANES, LANES), 0)
    dst = iota((2 * LANES, LANES), 1)
    seg = dst // OWN
    h_pack = one_hot(
        jnp.logical_and(seg < 3, src == seg * (ROWS * CB) + (ROWS - ITERS) * CB + dst - seg * OWN)
    )
    hops = []
    for b in [c] + others:
        if not hops:
            own.wait()
        else:
            send(sendbuf.at[b], piece.at[b], s_send.at[b], s_recv.at[b], comp=b).wait_recv()
        hsend[b] = mm(piece[b], h_pack).astype(BF16)
        hops.append(send(hsend.at[b], hrecv.at[b], h_send.at[b], h_recv.at[b], pts=down))
        hops[-1].start()

    u_src = iota((2 * LANES, 3 * LANES), 0)
    u_dst = iota((2 * LANES, 3 * LANES), 1)
    u_seg = u_dst // LANES
    u_lane = u_dst - u_seg * LANES
    own_lane = jnp.logical_and(u_lane >= OWN, u_lane < OWN + ROWS * CB)
    unpack = one_hot(jnp.logical_and(own_lane, u_src == u_seg * (ROWS * CB) + u_lane - OWN))
    hu_src = iota((LANES, 3 * LANES), 0)
    hu_dst = iota((LANES, 3 * LANES), 1)
    hu_seg = hu_dst // LANES
    hu_lane = hu_dst - hu_seg * LANES
    h_unpack = one_hot(jnp.logical_and(hu_lane < OWN, hu_src == hu_seg * OWN + hu_lane))
    for hop in hops:
        hop.wait_recv()
    for b in range(NB):
        full = mm(piece[b], unpack) + mm(hrecv[b], h_unpack)
        for t in range(3):
            size = min(SEG, LB - t * SEG)
            a = PAD + b * LB + t * SEG
            va[a : a + size, :] = full[:size, t * LANES : (t + 1) * LANES] * mexp[a : a + size, :]

    for it in range(ITERS):
        v, w = (va, vb) if it % 2 == 0 else (vb, va)
        v[PAD - 1 : PAD, :] = v[PAD + LON - 1 : PAD + LON, :]
        v[PAD + LON : PAD + LON + 1, :] = v[PAD : PAD + 1, :]
        for i in range(LON // step_rows):
            a = PAD + i * step_rows
            k = i * step_rows
            here = v[a : a + step_rows, :]
            side = jnp.where(east, v[a - 1 : a - 1 + step_rows, :], v[a + 1 : a + 1 + step_rows, :])
            new = kbuf[k : k + step_rows, :] * here + mexp[a : a + step_rows, :] * (
                ax * side + ay * pltpu.roll(here, CB, 1)
            )
            if it < ITERS - 1:
                w[a : a + step_rows, :] = new
            else:
                vfin[k : k + step_rows, :] = new.astype(BF16)

    for pair in range(ROWS // 2):
        both = mm(vfin[...], spread_matrix(OWN + 2 * pair * CB, GROUPS))
        tab[2 * pair * LON : (2 * pair + 1) * LON, :] = both[:, :LANES]
        tab[(2 * pair + 1) * LON : (2 * pair + 2) * LON, :] = both[:, LANES:]
    get_cells.wait()
    unroll = 23

    def fill_block(d):
        def rows(q, _):
            for u in range(unroll):
                r = q * unroll + u
                at = cells.at[pl.ds(d * (USED_ROWS * GROUPS) + r, (GROUPS - 1) * USED_ROWS + 1)]
                stage[pl.ds(r, 1), :] = merge_rows(tab, at, GROUPS, USED_ROWS, lane)
            return 0

        lax.fori_loop(0, USED_ROWS // unroll, rows, 0)

    stage[USED_ROWS:CAP_ROWS, :] = jnp.zeros((CAP_ROWS - USED_ROWS, LANES), F32)

    def owner(s, _):
        d = lax.rem(j + s, NB)
        fill_block(d)
        outgo[d] = stage[0:CAP_ROWS, :].astype(BF16)
        send(outgo.at[d], income.at[j], o_send.at[d], o_recv.at[j], pts=d).start()
        return 0

    lax.fori_loop(1, NB, owner, 0)
    fill_block(j)
    income[j] = stage[0:CAP_ROWS, :].astype(BF16)

    def arrive(s, _):
        d = lax.rem(j + s, NB)
        copy = send(outgo.at[d], income.at[d], o_send.at[d], o_recv.at[d], pts=d)
        copy.wait_send()
        copy.wait_recv()
        return 0

    lax.fori_loop(1, NB, arrive, 0)

    total = NB * CAP_ROWS
    got = income[...].reshape(total, LANES)
    for pair in range(GROUPS // 2):
        both = mm(got, spread_matrix(2 * pair * CB, SLOT_GROUPS))
        tab[2 * pair * total : (2 * pair + 1) * total, :] = both[:, :LANES]
        tab[(2 * pair + 1) * total : (2 * pair + 2) * total, :] = both[:, LANES:]
    get_slots.wait()
    slot_unroll = 16

    def slot_rows(q, _):
        for u in range(slot_unroll):
            r = q * slot_unroll + u
            at = slots.at[pl.ds(r, (SLOT_GROUPS - 1) * SLOT_ROWS + 1)]
            stage[pl.ds(r, 1), :] = merge_rows(tab, at, SLOT_GROUPS, SLOT_ROWS, lane)
        return 0

    lax.fori_loop(0, SLOT_ROWS // slot_unroll, slot_rows, 0)
    t_row = iota((SLOT_GROUPS * 16, LANES), 0)
    t_lane = iota((SLOT_GROUPS * 16, LANES), 1)
    group = t_row // 16
    comp = t_row - group * 16
    turn = one_hot(jnp.logical_and(comp < CB, t_lane == group * CB + comp))
    width = out_ref.shape[1]
    turned = lax.dot_general(
        turn, stage[...].astype(BF16), (((1,), (1,)), ((), ())), preferred_element_type=F32
    )
    for g in range(SLOT_GROUPS):
        size = min(SLOT_ROWS, width - g * SLOT_ROWS)
        out_ref[:, g * SLOT_ROWS : g * SLOT_ROWS + size] = turned[16 * g : 16 * g + CB, :size].astype(BF16)

    for copy in copies:
        copy.wait_send()
    for hop in hops:
        hop.wait_send()


def whole(x, mask, coef, cell_idx, slot_idx, width):
    dma = pltpu.SemaphoreType.DMA
    vmem = pl.BlockSpec(memory_space=pltpu.VMEM)
    hbm = pl.BlockSpec(memory_space=pltpu.HBM)
    wrapped = PAD + LON + 8
    return pl.pallas_call(
        whole_kernel,
        out_shape=jax.ShapeDtypeStruct((CB, width), BF16),
        in_specs=[vmem, hbm, vmem, hbm, hbm],
        out_specs=vmem,
        scratch_shapes=[
            pltpu.VMEM((NB, SEG, 2 * LANES), BF16),
            pltpu.VMEM((NB, SEG, 2 * LANES), BF16),
            pltpu.VMEM((NB, SEG, LANES), BF16),
            pltpu.VMEM((NB, SEG, LANES), BF16),
            pltpu.VMEM((3 * SEG, LANES), F32),
            pltpu.VMEM((ROWS, LON), jnp.int32),
            pltpu.VMEM((ROWS, LON), jnp.int32),
            pltpu.VMEM((ROWS, LON), jnp.int32),
            pltpu.VMEM((3 * ROWS, LON), F32),
            pltpu.VMEM((wrapped, LANES), F32),
            pltpu.VMEM((LON, LANES), F32),
            pltpu.VMEM((LON, LANES), F32),
            pltpu.VMEM((wrapped, LANES), F32),
            pltpu.VMEM((wrapped, LANES), F32),
            pltpu.VMEM((LON, LANES), BF16),
            pltpu.VMEM((ROWS * LON, LANES), F32),
            pltpu.VMEM((SLOT_ROWS, LANES), F32),
            pltpu.VMEM((NB, CAP_ROWS, LANES), BF16),
            pltpu.VMEM((NB, CAP_ROWS, LANES), BF16),
            pltpu.SMEM(cell_idx.shape, jnp.int32),
            pltpu.SMEM(slot_idx.shape, jnp.int32),
            dma((NB,)), dma((NB,)), dma((NB,)), dma((NB,)), dma((2,)), dma((2,)), dma((4,)),
            dma((NB,)), dma((NB,)),
        ],
        compiler_params=pltpu.CompilerParams(
            collective_id=0, has_side_effects=True, vmem_limit_bytes=52 << 20
        ),
        name="propagate_and_return",
    )(x, mask, coef, cell_idx, slot_idx)


def coefficients(comp_here, pts_here):
    grid_rows = ROWS * NB
    lane = jnp.arange(LANES, dtype=jnp.int32)
    rr = lane // CB
    comp = comp_here * CB + lane % CB
    quad = comp_here % 4
    north = quad < 2
    band_row = jnp.where(north, rr - ITERS, ROWS - 1 + ITERS - rr)
    row = (pts_here * ROWS + band_row).astype(F32)

    def cosines(row_ids):
        radians = (45.0 + 0.1 * (row_ids + 0.5 - 0.5 * grid_rows)) * (math.pi / 180.0)
        return jnp.cos(radians), jnp.cos(radians + 0.05 * math.pi / 180.0)

    cos_mid, cos_upper = cosines(row)
    cos_lower = cosines(row - 1.0)[1]
    freq = (comp // ND).astype(F32)
    angle = ((comp % ND).astype(F32) + 0.5) * (2.0 * math.pi / ND)
    top = math.cos((45.0 + 0.05 * grid_rows) * math.pi / 180.0)
    speed = 0.6 * top * jnp.power(jnp.float32(1.1), -freq)
    east_x = jnp.abs(speed * jnp.cos(angle))
    north_y = jnp.abs(speed * jnp.sin(angle))
    ax = east_x / cos_mid
    up = north_y * jnp.where(north, cos_lower, cos_upper) / cos_mid
    dn = north_y * jnp.where(north, cos_upper, cos_lower) / cos_mid
    live = rr < ROWS + ITERS
    rows = [jnp.where(live, value, 0.0) for value in (ax, up, dn)]
    return jnp.stack(rows + [jnp.zeros((LANES,), F32)] * 5)


def local(spectra, land_mask, send_rows, row_counts, return_index):
    comp_here = lax.axis_index("comp")
    pts_here = lax.axis_index("pts")
    north = comp_here % 4 < 2

    cells = send_rows[0]
    row = cells // LON
    cell_row = jnp.where(north, row, ROWS - 1 - row) * LON + cells - row * LON
    cell_idx = jnp.pad(cell_row, ((0, 0), (0, USED_ROWS * GROUPS - CAP))).reshape(-1)

    counts_in = lax.dynamic_slice_in_dim(row_counts, pts_here, 1, 1)[:, 0]
    offsets = jnp.cumsum(counts_in) - counts_in
    picked = return_index[0]
    source = jnp.sum((picked[:, None] >= offsets[None, :]).astype(jnp.int32), axis=1) - 1
    start = jnp.sum(
        jnp.where(source[:, None] == jnp.arange(NB, dtype=jnp.int32)[None, :], offsets[None, :], 0), axis=1
    )
    within = picked - start
    group = within // USED_ROWS
    slot = group * (NB * CAP_ROWS) + source * CAP_ROWS + within - group * USED_ROWS
    slot_idx = jnp.pad(slot, (0, SLOT_ROWS * SLOT_GROUPS - slot.shape[0]))
    coef = coefficients(comp_here, pts_here)
    return whole(spectra, land_mask, coef, cell_idx, slot_idx, picked.shape[0])


def solution(mesh):
    placed = (P("comp", "pts"), P("pts", None), P("pts", None, None), P(), P("pts", None))
    return jax.shard_map(
        local, mesh=mesh, in_specs=placed, out_specs=P("comp", "pts"), check_vma=False
    )
```

```python
import functools
import math

import jax
import jax.numpy as jnp
from jax import lax
from jax.experimental import pallas as pl
from jax.experimental.pallas import tpu as pltpu
from jax.sharding import PartitionSpec as P

ND = 36
ITERS = 4
LANES = 128
CB = 9
ROWS = 8
OWN = ITERS * CB
LON = 3600
LB = 225
SEG = 80
NB = 16
PAD = 8
GROUPS = 14
CAP = 1280
CAP_ROWS = 96
USED_ROWS = 92
SLOT_ROWS = 1024
SLOT_GROUPS = 13
F32 = jnp.float32
BF16 = jnp.bfloat16


def iota(shape, dim):
    return lax.broadcasted_iota(jnp.int32, shape, dim)


def one_hot(cond):
    return jnp.where(cond, 1.0, 0.0).astype(BF16)


def mm(a, b):
    return jnp.dot(a, b, preferred_element_type=F32)


def send(src, dst, send_sem, recv_sem, **where):
    return pltpu.make_async_remote_copy(
        src_ref=src, dst_ref=dst, send_sem=send_sem, recv_sem=recv_sem,
        device_id=where, device_id_type=pl.DeviceIdType.MESH,
    )


def merge_rows(tab, at, groups, stride, lane):
    row = tab[pl.ds(at[0], 1), :]
    for g in range(1, groups):
        row = jnp.where(lane >= CB * g, tab[pl.ds(at[g * stride], 1), :], row)
    return row


def spread_matrix(first, second, live):
    src = iota((LANES, 2 * LANES), 0)
    dst = iota((LANES, 2 * LANES), 1)
    half = dst // LANES
    lane2 = dst - half * LANES
    return one_hot(
        jnp.logical_and(lane2 < live * CB, src == jnp.where(half == 0, first, second) + lane2 - (lane2 // CB) * CB)
    )


def partners(c):
    z = c // 2
    order = [z * 2 + 1 - (c - z * 2)]
    for dist in (1, 2, 3, 4):
        for chip in (4,) if dist == 4 else (dist, 8 - dist):
            for core in range(2):
                order.append(lax.rem(z + chip, 8) * 2 + core)
    return order


def whole_kernel(
    x_ref, mask_ref, coef_ref, cell_ref, count_ref, back_ref, out_ref,
    xin, sendbuf, piece, hsend, hrecv, ymid, mprev, mown, mnext, mstack, mexp, mdown, kbuf, va, vb,
    vfin, tab, stage, outgo, income, back, slotv, cells, counts, slots,
    s_send, s_recv, h_send, h_recv, m_send, m_recv, l_sem, o_send, o_recv,
):
    c = lax.axis_index("comp")
    j = lax.axis_index("pts")
    nxt = lax.rem(j + 1, NB)
    prv = lax.rem(j + NB - 1, NB)
    quad = lax.rem(c, 4)
    north = quad < 2
    east = jnp.logical_or(quad == 0, quad == 3)
    down = jnp.where(north, nxt, prv)
    others = partners(c)

    barrier = pltpu.get_barrier_semaphore()
    for s in range(1, NB):
        pl.semaphore_signal(
            barrier, inc=1, device_id={"comp": lax.rem(c + s, NB)}, device_id_type=pl.DeviceIdType.MESH
        )
        pl.semaphore_signal(
            barrier, inc=1, device_id={"pts": lax.rem(j + s, NB)}, device_id_type=pl.DeviceIdType.MESH
        )
    get_x = pltpu.make_async_copy(x_ref, xin, l_sem.at[1])
    get_mask = pltpu.make_async_copy(mask_ref, mown, l_sem.at[2])
    get_counts = pltpu.make_async_copy(count_ref, counts, l_sem.at[3])
    get_back = pltpu.make_async_copy(back_ref, back, l_sem.at[4])
    get_cells = pltpu.make_async_copy(cell_ref, cells.at[pl.ds(0, NB * CAP)], l_sem.at[5])
    for get in (get_x, get_mask, get_counts, get_back, get_cells):
        get.start()
    ymid[LB : 3 * SEG, :] = jnp.zeros((3 * SEG - LB, LANES), F32)
    get_x.wait()
    get_mask.wait()
    pl.semaphore_wait(barrier, 2 * (NB - 1))

    m_id = iota((ROWS * NB * CB, LANES), 0)
    lane = iota((1, LANES), 1)
    pos = lane // CB
    lane_s = iota((SEG, LANES), 1)
    x = xin[...]
    copies = []
    for n, t in enumerate(others + [c]):
        row = jnp.where(lax.rem(t, 4) < 2, pos, ROWS - 1 - pos)
        want = jnp.where(lane < ROWS * CB, row * (NB * CB) + t * CB + lane - pos * CB, -1)
        ymid[0:LB, :] = mm(x, one_hot(m_id == want))
        y0 = ymid[0:SEG, :]
        y1 = pltpu.roll(ymid[SEG : 2 * SEG, :], 72, 1)
        y2 = pltpu.roll(ymid[2 * SEG : 3 * SEG, :], 16, 1)
        to = sendbuf if n < NB - 1 else piece
        to[t, :, 0:LANES] = jnp.where(lane_s < 72, y0, y1).astype(BF16)
        to[t, :, LANES : 2 * LANES] = jnp.where(lane_s < 16, y1, y2).astype(BF16)
        if n < NB - 1:
            copies.append(send(sendbuf.at[t], piece.at[c], s_send.at[t], s_recv.at[c], comp=t))
            copies[-1].start()
        if n == 1:
            m_up = send(mown, mprev, m_send.at[0], m_recv.at[0], pts=nxt)
            m_up.start()
            m_dn = send(mown, mnext, m_send.at[1], m_recv.at[1], pts=prv)
            m_dn.start()

    m_up.wait()
    m_dn.wait()
    mstack[0:ROWS, :] = jnp.where(j > 0, mprev[...], 0).astype(F32)
    mstack[ROWS : 2 * ROWS, :] = mown[...].astype(F32)
    mstack[2 * ROWS : 3 * ROWS, :] = jnp.where(j < NB - 1, mnext[...], 0).astype(F32)
    g_id = iota((3 * ROWS, LANES), 0)
    l_id = iota((3 * ROWS, LANES), 1)
    rr = l_id // CB
    live = rr < ROWS + ITERS
    e_here = one_hot(jnp.logical_and(live, g_id == jnp.where(north, rr + 4, 19 - rr)))
    e_down = one_hot(jnp.logical_and(live, g_id == jnp.where(north, rr + 5, 18 - rr)))
    e_both = jnp.concatenate([e_here, e_down], axis=1)
    stack = mstack[...].astype(BF16)
    both = lax.dot_general(stack, e_both, (((0,), (0,)), ((), ())), preferred_element_type=F32)
    mexp[PAD : PAD + LON, :] = both[:, :LANES]
    mdown[...] = both[:, LANES:]
    mexp[PAD - 1 : PAD, :] = mexp[PAD + LON - 1 : PAD + LON, :]
    mexp[PAD + LON : PAD + LON + 1, :] = mexp[PAD : PAD + 1, :]
    ax = coef_ref[0:1, :]
    ay = coef_ref[1:2, :]
    ad = coef_ref[2:3, :]
    step_rows = 120
    for i in range(LON // step_rows):
        a = PAD + i * step_rows
        m = mexp[a : a + step_rows, :]
        lon_down = jnp.where(
            east, mexp[a + 1 : a + 1 + step_rows, :], mexp[a - 1 : a - 1 + step_rows, :]
        )
        kbuf[i * step_rows : (i + 1) * step_rows, :] = m * (
            1.0 - ax * lon_down - ad * mdown[i * step_rows : (i + 1) * step_rows, :]
        )

    get_counts.wait()
    get_back.wait()
    width = out_ref.shape[1]
    offsets = [jnp.int32(0)]
    for i in range(NB - 1):
        offsets.append(offsets[-1] + counts[i, j])
    for a in range(0, width, SLOT_ROWS):
        size = min(SLOT_ROWS, width - a)
        picked = back[:, a : a + size]
        start = jnp.zeros_like(picked)
        place = jnp.zeros_like(picked)
        for i in range(1, NB):
            later = picked >= offsets[i]
            start = jnp.where(later, offsets[i], start)
            place = jnp.where(later, i * CAP_ROWS, place)
        within = picked - start
        place = place + within
        for g in range(1, GROUPS):
            place = place + jnp.where(within >= g * USED_ROWS, NB * CAP_ROWS - USED_ROWS, 0)
        slotv[:, a : a + size] = place
    slotv[:, width:] = jnp.zeros((1, SLOT_ROWS * SLOT_GROUPS - width), jnp.int32)
    put_slots = pltpu.make_async_copy(slotv, slots, l_sem.at[0])
    put_slots.start()
    for i in range(USED_ROWS * GROUPS - CAP):
        cells[NB * CAP + i] = 0

    src = iota((2 * LANES, LANES), 0)
    dst = iota((2 * LANES, LANES), 1)
    seg = dst // OWN
    h_pack = one_hot(
        jnp.logical_and(seg < 3, src == seg * (ROWS * CB) + (ROWS - ITERS) * CB + dst - seg * OWN)
    )
    hops = []
    for b in [c] + others:
        if hops:
            send(sendbuf.at[b], piece.at[b], s_send.at[b], s_recv.at[b], comp=b).wait_recv()
        hsend[b] = mm(piece[b], h_pack).astype(BF16)
        hops.append(send(hsend.at[b], hrecv.at[b], h_send.at[b], h_recv.at[b], pts=down))
        hops[-1].start()

    u_src = iota((2 * LANES, 3 * LANES), 0)
    u_dst = iota((2 * LANES, 3 * LANES), 1)
    u_seg = u_dst // LANES
    u_lane = u_dst - u_seg * LANES
    own_lane = jnp.logical_and(u_lane >= OWN, u_lane < OWN + ROWS * CB)
    unpack = one_hot(jnp.logical_and(own_lane, u_src == u_seg * (ROWS * CB) + u_lane - OWN))
    hu_src = iota((LANES, 3 * LANES), 0)
    hu_dst = iota((LANES, 3 * LANES), 1)
    hu_seg = hu_dst // LANES
    hu_lane = hu_dst - hu_seg * LANES
    h_unpack = one_hot(jnp.logical_and(hu_lane < OWN, hu_src == hu_seg * OWN + hu_lane))
    for hop in hops:
        hop.wait_recv()
    for b in range(NB):
        full = mm(piece[b], unpack) + mm(hrecv[b], h_unpack)
        for t in range(3):
            size = min(SEG, LB - t * SEG)
            a = PAD + b * LB + t * SEG
            va[a : a + size, :] = full[:size, t * LANES : (t + 1) * LANES] * mexp[a : a + size, :]

    for it in range(ITERS):
        v, w = (va, vb) if it % 2 == 0 else (vb, va)
        v[PAD - 1 : PAD, :] = v[PAD + LON - 1 : PAD + LON, :]
        v[PAD + LON : PAD + LON + 1, :] = v[PAD : PAD + 1, :]
        for i in range(LON // step_rows):
            a = PAD + i * step_rows
            k = i * step_rows
            here = v[a : a + step_rows, :]
            side = jnp.where(east, v[a - 1 : a - 1 + step_rows, :], v[a + 1 : a + 1 + step_rows, :])
            new = kbuf[k : k + step_rows, :] * here + mexp[a : a + step_rows, :] * (
                ax * side + ay * pltpu.roll(here, CB, 1)
            )
            if it < ITERS - 1:
                w[a : a + step_rows, :] = new
            else:
                vfin[k : k + step_rows, :] = new.astype(BF16)

    for pair in range(ROWS // 2):
        here = jnp.where(north, 2 * pair, ROWS - 1 - 2 * pair)
        then = jnp.where(north, 2 * pair + 1, ROWS - 2 - 2 * pair)
        both = mm(vfin[...], spread_matrix(OWN + here * CB, OWN + then * CB, GROUPS))
        tab[2 * pair * LON : (2 * pair + 1) * LON, :] = both[:, :LANES]
        tab[(2 * pair + 1) * LON : (2 * pair + 2) * LON, :] = both[:, LANES:]
    get_cells.wait()
    unroll = 23

    def fill_block(d):
        def rows(q, _):
            for u in range(unroll):
                r = q * unroll + u
                at = cells.at[pl.ds(d * CAP + r, (GROUPS - 1) * USED_ROWS + 1)]
                stage[pl.ds(r, 1), :] = merge_rows(tab, at, GROUPS, USED_ROWS, lane)
            return 0

        lax.fori_loop(0, USED_ROWS // unroll, rows, 0)

    stage[USED_ROWS:CAP_ROWS, :] = jnp.zeros((CAP_ROWS - USED_ROWS, LANES), F32)

    def owner(s, _):
        d = lax.rem(j + s, NB)
        fill_block(d)
        outgo[d] = stage[0:CAP_ROWS, :].astype(BF16)
        send(outgo.at[d], income.at[j], o_send.at[d], o_recv.at[j], pts=d).start()
        return 0

    lax.fori_loop(1, NB, owner, 0)
    fill_block(j)
    income[j] = stage[0:CAP_ROWS, :].astype(BF16)

    def arrive(s, _):
        d = lax.rem(j + s, NB)
        copy = send(outgo.at[d], income.at[d], o_send.at[d], o_recv.at[d], pts=d)
        copy.wait_send()
        copy.wait_recv()
        return 0

    lax.fori_loop(1, NB, arrive, 0)

    total = NB * CAP_ROWS
    got = income[...].reshape(total, LANES)
    for pair in range(GROUPS // 2):
        both = mm(got, spread_matrix(2 * pair * CB, (2 * pair + 1) * CB, SLOT_GROUPS))
        tab[2 * pair * total : (2 * pair + 1) * total, :] = both[:, :LANES]
        tab[(2 * pair + 1) * total : (2 * pair + 2) * total, :] = both[:, LANES:]
    put_slots.wait()
    slot_unroll = 16

    def slot_rows(q, _):
        for u in range(slot_unroll):
            r = q * slot_unroll + u
            at = slots.at[0, pl.ds(r, (SLOT_GROUPS - 1) * SLOT_ROWS + 1)]
            stage[pl.ds(r, 1), :] = merge_rows(tab, at, SLOT_GROUPS, SLOT_ROWS, lane)
        return 0

    lax.fori_loop(0, SLOT_ROWS // slot_unroll, slot_rows, 0)
    t_row = iota((SLOT_GROUPS * 16, LANES), 0)
    t_lane = iota((SLOT_GROUPS * 16, LANES), 1)
    group = t_row // 16
    comp = t_row - group * 16
    turn = one_hot(jnp.logical_and(comp < CB, t_lane == group * CB + comp))
    turned = lax.dot_general(
        turn, stage[...].astype(BF16), (((1,), (1,)), ((), ())), preferred_element_type=F32
    )
    for g in range(SLOT_GROUPS):
        size = min(SLOT_ROWS, width - g * SLOT_ROWS)
        out_ref[:, g * SLOT_ROWS : g * SLOT_ROWS + size] = turned[16 * g : 16 * g + CB, :size].astype(BF16)

    for copy in copies:
        copy.wait_send()
    for hop in hops:
        hop.wait_send()


def whole(x, mask, coef, cells, counts, back):
    dma = pltpu.SemaphoreType.DMA
    vmem = pl.BlockSpec(memory_space=pltpu.VMEM)
    hbm = pl.BlockSpec(memory_space=pltpu.HBM)
    wrapped = PAD + LON + 8
    return pl.pallas_call(
        whole_kernel,
        out_shape=jax.ShapeDtypeStruct((CB, back.shape[1]), BF16),
        in_specs=[hbm, hbm, vmem, hbm, hbm, hbm],
        out_specs=vmem,
        scratch_shapes=[
            pltpu.VMEM(x.shape, BF16),
            pltpu.VMEM((NB, SEG, 2 * LANES), BF16),
            pltpu.VMEM((NB, SEG, 2 * LANES), BF16),
            pltpu.VMEM((NB, SEG, LANES), BF16),
            pltpu.VMEM((NB, SEG, LANES), BF16),
            pltpu.VMEM((3 * SEG, LANES), F32),
            pltpu.VMEM((ROWS, LON), jnp.int32),
            pltpu.VMEM((ROWS, LON), jnp.int32),
            pltpu.VMEM((ROWS, LON), jnp.int32),
            pltpu.VMEM((3 * ROWS, LON), F32),
            pltpu.VMEM((wrapped, LANES), F32),
            pltpu.VMEM((LON, LANES), F32),
            pltpu.VMEM((LON, LANES), F32),
            pltpu.VMEM((wrapped, LANES), F32),
            pltpu.VMEM((wrapped, LANES), F32),
            pltpu.VMEM((LON, LANES), BF16),
            pltpu.VMEM((ROWS * LON, LANES), F32),
            pltpu.VMEM((SLOT_ROWS, LANES), F32),
            pltpu.VMEM((NB, CAP_ROWS, LANES), BF16),
            pltpu.VMEM((NB, CAP_ROWS, LANES), BF16),
            pltpu.VMEM(back.shape, jnp.int32),
            pltpu.VMEM((1, SLOT_ROWS * SLOT_GROUPS), jnp.int32),
            pltpu.SMEM((NB * CAP + USED_ROWS * GROUPS - CAP,), jnp.int32),
            pltpu.SMEM((NB, NB), jnp.int32),
            pltpu.SMEM((1, SLOT_ROWS * SLOT_GROUPS), jnp.int32),
            dma((NB,)), dma((NB,)), dma((NB,)), dma((NB,)), dma((2,)), dma((2,)), dma((6,)),
            dma((NB,)), dma((NB,)),
        ],
        compiler_params=pltpu.CompilerParams(
            collective_id=0, has_side_effects=True, vmem_limit_bytes=52 << 20
        ),
        name="propagate_and_return",
    )(x, mask, coef, cells, counts, back)


def coefficients(comp_here, pts_here):
    grid_rows = ROWS * NB
    lane = jnp.arange(LANES, dtype=jnp.int32)
    rr = lane // CB
    comp = comp_here * CB + lane % CB
    quad = comp_here % 4
    north = quad < 2
    band_row = jnp.where(north, rr - ITERS, ROWS - 1 + ITERS - rr)
    row = (pts_here * ROWS + band_row).astype(F32)

    def cosines(row_ids):
        radians = (45.0 + 0.1 * (row_ids + 0.5 - 0.5 * grid_rows)) * (math.pi / 180.0)
        return jnp.cos(radians), jnp.cos(radians + 0.05 * math.pi / 180.0)

    cos_mid, cos_upper = cosines(row)
    cos_lower = cosines(row - 1.0)[1]
    freq = (comp // ND).astype(F32)
    angle = ((comp % ND).astype(F32) + 0.5) * (2.0 * math.pi / ND)
    top = math.cos((45.0 + 0.05 * grid_rows) * math.pi / 180.0)
    speed = 0.6 * top * jnp.power(jnp.float32(1.1), -freq)
    east_x = jnp.abs(speed * jnp.cos(angle))
    north_y = jnp.abs(speed * jnp.sin(angle))
    ax = east_x / cos_mid
    up = north_y * jnp.where(north, cos_lower, cos_upper) / cos_mid
    dn = north_y * jnp.where(north, cos_upper, cos_lower) / cos_mid
    live = rr < ROWS + ITERS
    rows = [jnp.where(live, value, 0.0) for value in (ax, up, dn)]
    return jnp.stack(rows + [jnp.zeros((LANES,), F32)] * 5)


def local(spectra, land_mask, send_rows, row_counts, return_index):
    comp_here = lax.axis_index("comp")
    pts_here = lax.axis_index("pts")
    coef = coefficients(comp_here, pts_here)
    return whole(spectra, land_mask, coef, send_rows.reshape(-1), row_counts, return_index)


def solution(mesh):
    placed = (P("comp", "pts"), P("pts", None), P("pts", None, None), P(), P("pts", None))
    return jax.shard_map(
        local, mesh=mesh, in_specs=placed, out_specs=P("comp", "pts"), check_vma=False
    )
```

```python
import functools
import math

import jax
import jax.numpy as jnp
from jax import lax
from jax.experimental import pallas as pl
from jax.experimental.pallas import tpu as pltpu
from jax.sharding import PartitionSpec as P

ND = 36
ITERS = 4
LANES = 128
CB = 9
ROWS = 8
OWN = ITERS * CB
LON = 3600
LB = 225
SEG = 80
NB = 16
PAD = 8
GROUPS = 14
CAP = 1280
CAP_ROWS = 96
USED_ROWS = 92
PAIR_GROUPS = 7
CELLS = 2048
CHUNK = 720
SLOT_ROWS = 1024
SLOT_GROUPS = 13
F32 = jnp.float32
BF16 = jnp.bfloat16


def iota(shape, dim):
    return lax.broadcasted_iota(jnp.int32, shape, dim)


def one_hot(cond):
    return jnp.where(cond, 1.0, 0.0).astype(BF16)


def mm(a, b):
    return jnp.dot(a, b, preferred_element_type=F32)


def send(src, dst, send_sem, recv_sem, **where):
    return pltpu.make_async_remote_copy(
        src_ref=src, dst_ref=dst, send_sem=send_sem, recv_sem=recv_sem,
        device_id=where, device_id_type=pl.DeviceIdType.MESH,
    )


def merge_rows(tab, at, groups, stride, lane, width=CB):
    row = tab[pl.ds(at[0], 1), :]
    for g in range(1, groups):
        row = jnp.where(lane >= width * g, tab[pl.ds(at[g * stride], 1), :], row)
    return row


def spread_matrix(first, second, live):
    src = iota((LANES, 2 * LANES), 0)
    dst = iota((LANES, 2 * LANES), 1)
    half = dst // LANES
    lane2 = dst - half * LANES
    return one_hot(
        jnp.logical_and(lane2 < live * CB, src == jnp.where(half == 0, first, second) + lane2 - (lane2 // CB) * CB)
    )


def partners(c):
    z = c // 2
    order = [z * 2 + 1 - (c - z * 2)]
    for dist in (1, 2, 3, 4):
        for chip in (4,) if dist == 4 else (dist, 8 - dist):
            for core in range(2):
                order.append(lax.rem(z + chip, 8) * 2 + core)
    return order


def whole_kernel(
    x_ref, mask_ref, coef_ref, cell_ref, count_ref, back_ref, out_ref,
    xin, sendbuf, piece, hsend, hrecv, ymid, mprev, mown, mnext, mstack, mexp, mdown, kbuf, va, vb,
    vfin, vmate, tab, stage, outgo, income, back, slotv, cells, counts, slots,
    s_send, s_recv, h_send, h_recv, m_send, m_recv, l_sem, c_sem, v_send, v_recv, o_send, o_recv,
):
    c = lax.axis_index("comp")
    j = lax.axis_index("pts")
    nxt = lax.rem(j + 1, NB)
    prv = lax.rem(j + NB - 1, NB)
    quad = lax.rem(c, 4)
    north = quad < 2
    east = jnp.logical_or(quad == 0, quad == 3)
    down = jnp.where(north, nxt, prv)
    others = partners(c)
    core = lax.rem(c, 2)
    mate = c + 1 - 2 * core

    barrier = pltpu.get_barrier_semaphore()
    for s in range(1, NB):
        pl.semaphore_signal(
            barrier, inc=1, device_id={"comp": lax.rem(c + s, NB)}, device_id_type=pl.DeviceIdType.MESH
        )
        pl.semaphore_signal(
            barrier, inc=1, device_id={"pts": lax.rem(j + s, NB)}, device_id_type=pl.DeviceIdType.MESH
        )
        pl.semaphore_signal(
            barrier, inc=1, device_id={"comp": mate, "pts": lax.rem(j + s, NB)},
            device_id_type=pl.DeviceIdType.MESH,
        )
    get_x = pltpu.make_async_copy(x_ref, xin, l_sem.at[1])
    get_mask = pltpu.make_async_copy(mask_ref, mown, l_sem.at[2])
    get_counts = pltpu.make_async_copy(count_ref, counts, l_sem.at[3])
    get_back = pltpu.make_async_copy(back_ref, back, l_sem.at[4])
    get_cells = [
        pltpu.make_async_copy(cell_ref.at[0, i], cells.at[pl.ds(i * CELLS, CAP)], c_sem.at[i]) for i in range(NB)
    ]
    for get in [get_x, get_mask, get_counts, get_back] + get_cells:
        get.start()
    ymid[LB : 3 * SEG, :] = jnp.zeros((3 * SEG - LB, LANES), F32)
    get_x.wait()
    get_mask.wait()
    pl.semaphore_wait(barrier, 3 * (NB - 1))

    m_id = iota((ROWS * NB * CB, LANES), 0)
    lane = iota((1, LANES), 1)
    pos = lane // CB
    lane_s = iota((SEG, LANES), 1)
    x = xin[...]
    copies = []
    for n, t in enumerate(others + [c]):
        row = jnp.where(lax.rem(t, 4) < 2, pos, ROWS - 1 - pos)
        want = jnp.where(lane < ROWS * CB, row * (NB * CB) + t * CB + lane - pos * CB, -1)
        ymid[0:LB, :] = mm(x, one_hot(m_id == want))
        y0 = ymid[0:SEG, :]
        y1 = pltpu.roll(ymid[SEG : 2 * SEG, :], 72, 1)
        y2 = pltpu.roll(ymid[2 * SEG : 3 * SEG, :], 16, 1)
        to = sendbuf if n < NB - 1 else piece
        to[t, :, 0:LANES] = jnp.where(lane_s < 72, y0, y1).astype(BF16)
        to[t, :, LANES : 2 * LANES] = jnp.where(lane_s < 16, y1, y2).astype(BF16)
        if n < NB - 1:
            copies.append(send(sendbuf.at[t], piece.at[c], s_send.at[t], s_recv.at[c], comp=t))
            copies[-1].start()
        if n == 1:
            m_up = send(mown, mprev, m_send.at[0], m_recv.at[0], pts=nxt)
            m_up.start()
            m_dn = send(mown, mnext, m_send.at[1], m_recv.at[1], pts=prv)
            m_dn.start()

    m_up.wait()
    m_dn.wait()
    mstack[0:ROWS, :] = jnp.where(j > 0, mprev[...], 0).astype(F32)
    mstack[ROWS : 2 * ROWS, :] = mown[...].astype(F32)
    mstack[2 * ROWS : 3 * ROWS, :] = jnp.where(j < NB - 1, mnext[...], 0).astype(F32)
    g_id = iota((3 * ROWS, LANES), 0)
    l_id = iota((3 * ROWS, LANES), 1)
    rr = l_id // CB
    live = rr < ROWS + ITERS
    e_here = one_hot(jnp.logical_and(live, g_id == jnp.where(north, rr + 4, 19 - rr)))
    e_down = one_hot(jnp.logical_and(live, g_id == jnp.where(north, rr + 5, 18 - rr)))
    e_both = jnp.concatenate([e_here, e_down], axis=1)
    stack = mstack[...].astype(BF16)
    both = lax.dot_general(stack, e_both, (((0,), (0,)), ((), ())), preferred_element_type=F32)
    mexp[PAD : PAD + LON, :] = both[:, :LANES]
    mdown[...] = both[:, LANES:]
    mexp[PAD - 1 : PAD, :] = mexp[PAD + LON - 1 : PAD + LON, :]
    mexp[PAD + LON : PAD + LON + 1, :] = mexp[PAD : PAD + 1, :]
    ax = coef_ref[0:1, :]
    ay = coef_ref[1:2, :]
    ad = coef_ref[2:3, :]
    step_rows = 120
    for i in range(LON // step_rows):
        a = PAD + i * step_rows
        m = mexp[a : a + step_rows, :]
        lon_down = jnp.where(
            east, mexp[a + 1 : a + 1 + step_rows, :], mexp[a - 1 : a - 1 + step_rows, :]
        )
        kbuf[i * step_rows : (i + 1) * step_rows, :] = m * (
            1.0 - ax * lon_down - ad * mdown[i * step_rows : (i + 1) * step_rows, :]
        )

    get_counts.wait()
    get_back.wait()
    width = out_ref.shape[1]
    offsets = [jnp.int32(0)]
    for i in range(NB - 1):
        offsets.append(offsets[-1] + counts[i, j])
    for a in range(0, width, SLOT_ROWS):
        size = min(SLOT_ROWS, width - a)
        picked = back[:, a : a + size]
        start = jnp.zeros_like(picked)
        place = jnp.zeros_like(picked)
        for i in range(1, NB):
            later = picked >= offsets[i]
            start = jnp.where(later, offsets[i], start)
            place = jnp.where(later, i * CAP_ROWS, place)
        within = picked - start
        place = place + within
        for g in range(1, GROUPS):
            place = place + jnp.where(within >= g * USED_ROWS, NB * CAP_ROWS - USED_ROWS, 0)
        slotv[:, a : a + size] = place
    slotv[:, width:] = jnp.zeros((1, SLOT_ROWS * SLOT_GROUPS - width), jnp.int32)
    put_slots = pltpu.make_async_copy(slotv, slots, l_sem.at[0])
    put_slots.start()
    for i, get in enumerate(get_cells):
        get.wait()
        for k in range(CAP, USED_ROWS * GROUPS):
            cells[i * CELLS + k] = 0

    src = iota((2 * LANES, LANES), 0)
    dst = iota((2 * LANES, LANES), 1)
    seg = dst // OWN
    h_pack = one_hot(
        jnp.logical_and(seg < 3, src == seg * (ROWS * CB) + (ROWS - ITERS) * CB + dst - seg * OWN)
    )
    hops = []
    for b in [c] + others:
        if hops:
            send(sendbuf.at[b], piece.at[b], s_send.at[b], s_recv.at[b], comp=b).wait_recv()
        hsend[b] = mm(piece[b], h_pack).astype(BF16)
        hops.append(send(hsend.at[b], hrecv.at[b], h_send.at[b], h_recv.at[b], pts=down))
        hops[-1].start()

    u_src = iota((2 * LANES, 3 * LANES), 0)
    u_dst = iota((2 * LANES, 3 * LANES), 1)
    u_seg = u_dst // LANES
    u_lane = u_dst - u_seg * LANES
    own_lane = jnp.logical_and(u_lane >= OWN, u_lane < OWN + ROWS * CB)
    unpack = one_hot(jnp.logical_and(own_lane, u_src == u_seg * (ROWS * CB) + u_lane - OWN))
    hu_src = iota((LANES, 3 * LANES), 0)
    hu_dst = iota((LANES, 3 * LANES), 1)
    hu_seg = hu_dst // LANES
    hu_lane = hu_dst - hu_seg * LANES
    h_unpack = one_hot(jnp.logical_and(hu_lane < OWN, hu_src == hu_seg * OWN + hu_lane))
    for hop in hops:
        hop.wait_recv()
    for b in range(NB):
        full = mm(piece[b], unpack) + mm(hrecv[b], h_unpack)
        for t in range(3):
            size = min(SEG, LB - t * SEG)
            a = PAD + b * LB + t * SEG
            va[a : a + size, :] = full[:size, t * LANES : (t + 1) * LANES] * mexp[a : a + size, :]

    shares = []
    for it in range(ITERS):
        v, w = (va, vb) if it % 2 == 0 else (vb, va)
        v[PAD - 1 : PAD, :] = v[PAD + LON - 1 : PAD + LON, :]
        v[PAD + LON : PAD + LON + 1, :] = v[PAD : PAD + 1, :]
        for i in range(LON // step_rows):
            a = PAD + i * step_rows
            k = i * step_rows
            here = v[a : a + step_rows, :]
            side = jnp.where(east, v[a - 1 : a - 1 + step_rows, :], v[a + 1 : a + 1 + step_rows, :])
            new = kbuf[k : k + step_rows, :] * here + mexp[a : a + step_rows, :] * (
                ax * side + ay * pltpu.roll(here, CB, 1)
            )
            if it < ITERS - 1:
                w[a : a + step_rows, :] = new
            else:
                vfin[k : k + step_rows, :] = new.astype(BF16)
                if (k + step_rows) % CHUNK == 0:
                    n = k // CHUNK
                    part = pl.ds(n * CHUNK, CHUNK)
                    shares.append(send(vfin.at[part], vmate.at[part], v_send.at[n], v_recv.at[n], comp=mate))
                    shares[-1].start()

    spreads = []
    for pair in range(ROWS // 2):
        src = iota((2 * LANES, 2 * LANES), 0)
        dst = iota((2 * LANES, 2 * LANES), 1)
        half = dst // LANES
        lane2 = dst - half * LANES
        part = lane2 - (lane2 // (2 * CB)) * (2 * CB)
        of = part // CB
        here = jnp.where(north, 2 * pair, ROWS - 1 - 2 * pair)
        then = jnp.where(north, 2 * pair + 1, ROWS - 2 - 2 * pair)
        first = OWN + jnp.where(half == 0, here, then) * CB + jnp.where(of == core, 0, LANES)
        spreads.append(
            one_hot(jnp.logical_and(lane2 < PAIR_GROUPS * 2 * CB, src == first + part - of * CB))
        )
    for n, share in enumerate(shares):
        share.wait_recv()
        part = slice(n * CHUNK, (n + 1) * CHUNK)
        values = jnp.concatenate([vfin[part, :], vmate[part, :]], axis=1)
        for pair in range(ROWS // 2):
            both = mm(values, spreads[pair])
            a = 2 * pair * LON + n * CHUNK
            tab[a : a + CHUNK, :] = both[:, :LANES]
            tab[a + LON : a + LON + CHUNK, :] = both[:, LANES:]
    unroll = 23
    c_src = iota((2 * LANES, 2 * LANES), 0)
    c_dst = iota((2 * LANES, 2 * LANES), 1)
    c_core = c_dst // LANES
    c_lane = c_dst - c_core * LANES
    c_group = c_lane // CB
    c_half = lax.rem(c_group, 2)
    c_want = c_half * LANES + (c_group // 2) * (2 * CB) + c_core * CB + c_lane - c_group * CB
    cut = one_hot(jnp.logical_and(c_group < GROUPS, c_src == c_want))
    stage[USED_ROWS:CAP_ROWS, :] = jnp.zeros((CAP_ROWS - USED_ROWS, LANES), F32)
    stage[CAP_ROWS + USED_ROWS : 2 * CAP_ROWS, :] = jnp.zeros((CAP_ROWS - USED_ROWS, LANES), F32)
    stride = 2 * USED_ROWS

    def block_to(d, n):
        return send(
            outgo.at[d, n], income.at[j], o_send.at[d, n], o_recv.at[j],
            comp=c - core + n, pts=d,
        )

    def owner(s, _):
        d = lax.rem(j + 2 * lax.rem(s, NB // 2) + core, NB)
        for half in range(2):

            def rows(q, _, half=half):
                for u in range(unroll):
                    r = q * unroll + u
                    at = cells.at[pl.ds(d * CELLS + half * USED_ROWS + r, (PAIR_GROUPS - 1) * stride + 1)]
                    stage[pl.ds(half * CAP_ROWS + r, 1), :] = merge_rows(
                        tab, at, PAIR_GROUPS, stride, lane, 2 * CB
                    )
                return 0

            lax.fori_loop(0, USED_ROWS // unroll, rows, 0)
        packed = jnp.concatenate([stage[0:CAP_ROWS, :], stage[CAP_ROWS : 2 * CAP_ROWS, :]], axis=1)
        blocks = mm(packed.astype(BF16), cut).astype(BF16)

        @pl.when(d != j)
        def _():
            for n in range(2):
                outgo[d, n] = blocks[:, n * LANES : (n + 1) * LANES]
                block_to(d, n).start()

        @pl.when(d == j)
        def _():
            income[j] = blocks[:, :LANES]
            outgo[d, 1] = blocks[:, LANES:]
            block_to(d, 1).start()

        return 0

    lax.fori_loop(1, NB // 2 + 1, owner, 0)

    def sent(s, _):
        d = lax.rem(j + 2 * s + core, NB)
        block_to(d, 1).wait_send()

        @pl.when(d != j)
        def _():
            block_to(d, 0).wait_send()

        return 0

    lax.fori_loop(0, NB // 2, sent, 0)

    def arrive(s, _):
        d = lax.rem(j + s, NB)

        @pl.when(jnp.logical_or(s > 0, core == 1))
        def _():
            send(
                outgo.at[d, 0], income.at[d], o_send.at[d, 0], o_recv.at[d], comp=mate, pts=d
            ).wait_recv()

        return 0

    lax.fori_loop(0, NB, arrive, 0)

    total = NB * CAP_ROWS
    got = income[...].reshape(total, LANES)
    for pair in range(GROUPS // 2):
        both = mm(got, spread_matrix(2 * pair * CB, (2 * pair + 1) * CB, SLOT_GROUPS))
        tab[2 * pair * total : (2 * pair + 1) * total, :] = both[:, :LANES]
        tab[(2 * pair + 1) * total : (2 * pair + 2) * total, :] = both[:, LANES:]
    put_slots.wait()
    slot_unroll = 16

    def slot_rows(q, _):
        for u in range(slot_unroll):
            r = q * slot_unroll + u
            at = slots.at[0, pl.ds(r, (SLOT_GROUPS - 1) * SLOT_ROWS + 1)]
            stage[pl.ds(r, 1), :] = merge_rows(tab, at, SLOT_GROUPS, SLOT_ROWS, lane)
        return 0

    lax.fori_loop(0, SLOT_ROWS // slot_unroll, slot_rows, 0)
    t_row = iota((SLOT_GROUPS * 16, LANES), 0)
    t_lane = iota((SLOT_GROUPS * 16, LANES), 1)
    group = t_row // 16
    comp = t_row - group * 16
    turn = one_hot(jnp.logical_and(comp < CB, t_lane == group * CB + comp))
    turned = lax.dot_general(
        turn, stage[...].astype(BF16), (((1,), (1,)), ((), ())), preferred_element_type=F32
    )
    for g in range(SLOT_GROUPS):
        size = min(SLOT_ROWS, width - g * SLOT_ROWS)
        out_ref[:, g * SLOT_ROWS : g * SLOT_ROWS + size] = turned[16 * g : 16 * g + CB, :size].astype(BF16)

    for copy in copies + shares:
        copy.wait_send()
    for hop in hops:
        hop.wait_send()


def whole(x, mask, coef, cells, counts, back):
    dma = pltpu.SemaphoreType.DMA
    vmem = pl.BlockSpec(memory_space=pltpu.VMEM)
    hbm = pl.BlockSpec(memory_space=pltpu.HBM)
    wrapped = PAD + LON + 8
    return pl.pallas_call(
        whole_kernel,
        out_shape=jax.ShapeDtypeStruct((CB, back.shape[1]), BF16),
        in_specs=[hbm, hbm, vmem, hbm, hbm, hbm],
        out_specs=vmem,
        scratch_shapes=[
            pltpu.VMEM(x.shape, BF16),
            pltpu.VMEM((NB, SEG, 2 * LANES), BF16),
            pltpu.VMEM((NB, SEG, 2 * LANES), BF16),
            pltpu.VMEM((NB, SEG, LANES), BF16),
            pltpu.VMEM((NB, SEG, LANES), BF16),
            pltpu.VMEM((3 * SEG, LANES), F32),
            pltpu.VMEM((ROWS, LON), jnp.int32),
            pltpu.VMEM((ROWS, LON), jnp.int32),
            pltpu.VMEM((ROWS, LON), jnp.int32),
            pltpu.VMEM((3 * ROWS, LON), F32),
            pltpu.VMEM((wrapped, LANES), F32),
            pltpu.VMEM((LON, LANES), F32),
            pltpu.VMEM((LON, LANES), F32),
            pltpu.VMEM((wrapped, LANES), F32),
            pltpu.VMEM((wrapped, LANES), F32),
            pltpu.VMEM((LON, LANES), BF16),
            pltpu.VMEM((LON, LANES), BF16),
            pltpu.VMEM((ROWS * LON, LANES), F32),
            pltpu.VMEM((SLOT_ROWS, LANES), F32),
            pltpu.VMEM((NB, 2, CAP_ROWS, LANES), BF16),
            pltpu.VMEM((NB, CAP_ROWS, LANES), BF16),
            pltpu.VMEM(back.shape, jnp.int32),
            pltpu.VMEM((1, SLOT_ROWS * SLOT_GROUPS), jnp.int32),
            pltpu.SMEM((NB * CELLS,), jnp.int32),
            pltpu.SMEM((NB, NB), jnp.int32),
            pltpu.SMEM((1, SLOT_ROWS * SLOT_GROUPS), jnp.int32),
            dma((NB,)), dma((NB,)), dma((NB,)), dma((NB,)), dma((2,)), dma((2,)), dma((6,)), dma((NB,)),
            dma((LON // CHUNK,)), dma((LON // CHUNK,)), dma((NB, 2)), dma((NB,)),
        ],
        compiler_params=pltpu.CompilerParams(
            collective_id=0, has_side_effects=True, vmem_limit_bytes=60 << 20
        ),
        name="propagate_and_return",
    )(x, mask, coef, cells, counts, back)


def coefficients(comp_here, pts_here):
    grid_rows = ROWS * NB
    lane = jnp.arange(LANES, dtype=jnp.int32)
    rr = lane // CB
    comp = comp_here * CB + lane % CB
    quad = comp_here % 4
    north = quad < 2
    band_row = jnp.where(north, rr - ITERS, ROWS - 1 + ITERS - rr)
    row = (pts_here * ROWS + band_row).astype(F32)

    def cosines(row_ids):
        radians = (45.0 + 0.1 * (row_ids + 0.5 - 0.5 * grid_rows)) * (math.pi / 180.0)
        return jnp.cos(radians), jnp.cos(radians + 0.05 * math.pi / 180.0)

    cos_mid, cos_upper = cosines(row)
    cos_lower = cosines(row - 1.0)[1]
    freq = (comp // ND).astype(F32)
    angle = ((comp % ND).astype(F32) + 0.5) * (2.0 * math.pi / ND)
    top = math.cos((45.0 + 0.05 * grid_rows) * math.pi / 180.0)
    speed = 0.6 * top * jnp.power(jnp.float32(1.1), -freq)
    east_x = jnp.abs(speed * jnp.cos(angle))
    north_y = jnp.abs(speed * jnp.sin(angle))
    ax = east_x / cos_mid
    up = north_y * jnp.where(north, cos_lower, cos_upper) / cos_mid
    dn = north_y * jnp.where(north, cos_upper, cos_lower) / cos_mid
    live = rr < ROWS + ITERS
    rows = [jnp.where(live, value, 0.0) for value in (ax, up, dn)]
    return jnp.stack(rows + [jnp.zeros((LANES,), F32)] * 5)


def local(spectra, land_mask, send_rows, row_counts, return_index):
    comp_here = lax.axis_index("comp")
    pts_here = lax.axis_index("pts")
    coef = coefficients(comp_here, pts_here)
    return whole(spectra, land_mask, coef, send_rows, row_counts, return_index)


def solution(mesh):
    placed = (P("comp", "pts"), P("pts", None), P("pts", None, None), P(), P("pts", None))
    return jax.shard_map(
        local, mesh=mesh, in_specs=placed, out_specs=P("comp", "pts"), check_vma=False
    )
```

```python
import functools
import math

import jax
import jax.numpy as jnp
from jax import lax
from jax.experimental import pallas as pl
from jax.experimental.pallas import tpu as pltpu
from jax.sharding import PartitionSpec as P

ND = 36
ITERS = 4
LANES = 128
CB = 9
ROWS = 8
OWN = ITERS * CB
LON = 3600
LB = 225
SEG = 80
NB = 16
PAD = 16
GROUPS = 14
CAP = 1280
CAP_ROWS = 96
USED_ROWS = 92
PAIR_GROUPS = 7
CELLS = 2048
CHUNK = 720
SLOT_ROWS = 1024
SLOT_GROUPS = 13
F32 = jnp.float32
BF16 = jnp.bfloat16


def iota(shape, dim):
    return lax.broadcasted_iota(jnp.int32, shape, dim)


def one_hot(cond):
    return jnp.where(cond, 1.0, 0.0).astype(BF16)


def mm(a, b):
    return jnp.dot(a, b, preferred_element_type=F32)


def send(src, dst, send_sem, recv_sem, **where):
    return pltpu.make_async_remote_copy(
        src_ref=src, dst_ref=dst, send_sem=send_sem, recv_sem=recv_sem,
        device_id=where, device_id_type=pl.DeviceIdType.MESH,
    )


def merge_rows(tab, at, groups, stride, lane, width=CB):
    row = tab[pl.ds(at[0], 1), :]
    for g in range(1, groups):
        row = jnp.where(lane >= width * g, tab[pl.ds(at[g * stride], 1), :], row)
    return row


def spread_matrix(first, second, live):
    src = iota((LANES, 2 * LANES), 0)
    dst = iota((LANES, 2 * LANES), 1)
    half = dst // LANES
    lane2 = dst - half * LANES
    return one_hot(
        jnp.logical_and(lane2 < live * CB, src == jnp.where(half == 0, first, second) + lane2 - (lane2 // CB) * CB)
    )


def wrap(ref):
    ref[0:PAD, :] = ref[LON : LON + PAD, :]
    ref[PAD + LON : 2 * PAD + LON, :] = ref[PAD : 2 * PAD, :]


def partners(c):
    z = c // 2
    order = [z * 2 + 1 - (c - z * 2)]
    for dist in (1, 2, 3, 4):
        for chip in (4,) if dist == 4 else (dist, 8 - dist):
            for core in range(2):
                order.append(lax.rem(z + chip, 8) * 2 + core)
    return order


def whole_kernel(
    x_ref, mask_ref, coef_ref, cell_ref, count_ref, back_ref, out_ref,
    xin, sendbuf, piece, hsend, hrecv, ymid, mprev, mown, mnext, mstack, mexp, mdown, kbuf, va, vb, vc,
    vfin, vmate, tab, stage_a, stage_b, stage, outgo, income, back, slotv, cells, counts, slots,
    s_send, s_recv, h_send, h_recv, m_send, m_recv, l_sem, c_sem, v_send, v_recv, o_send, o_recv,
):
    c = lax.axis_index("comp")
    j = lax.axis_index("pts")
    nxt = lax.rem(j + 1, NB)
    prv = lax.rem(j + NB - 1, NB)
    quad = lax.rem(c, 4)
    north = quad < 2
    east = jnp.logical_or(quad == 0, quad == 3)
    down = jnp.where(north, nxt, prv)
    others = partners(c)
    core = lax.rem(c, 2)
    mate = c + 1 - 2 * core

    get_x = pltpu.make_async_copy(x_ref, xin, l_sem.at[1])
    get_mask = pltpu.make_async_copy(mask_ref, mown, l_sem.at[2])
    get_x.start()
    get_mask.start()

    barrier = pltpu.get_barrier_semaphore()

    def greet(**where):
        pl.semaphore_signal(barrier, inc=1, device_id=where, device_id_type=pl.DeviceIdType.MESH)

    for other in others:
        greet(comp=other)
    greet(pts=nxt)
    greet(pts=prv)
    for s in range(1, NB):
        greet(comp=c - core + s % 2, pts=lax.rem(j + NB - s, NB))
    get_counts = pltpu.make_async_copy(count_ref, counts, l_sem.at[3])
    get_back = pltpu.make_async_copy(back_ref, back, l_sem.at[4])
    get_cells = [
        pltpu.make_async_copy(cell_ref.at[0, i], cells.at[pl.ds(i * CELLS, CAP)], c_sem.at[i]) for i in range(NB)
    ]
    for n in range(2):
        ymid[n, LB : 3 * SEG, :] = jnp.zeros((3 * SEG - LB, 2 * LANES), F32)
    get_x.wait()
    get_mask.wait()
    pl.semaphore_wait(barrier, NB + 1 + NB - 2 + 2 * core)

    m_id = iota((ROWS * NB * CB, 2 * LANES), 0)
    lane = iota((1, LANES), 1)
    lane_2 = iota((1, 2 * LANES), 1)
    lane_c = lane_2 // LANES
    lane_1 = lane_2 - lane_c * LANES
    pos = lane_1 // CB
    lane_s = iota((SEG, LANES), 1)
    x = xin[...]
    copies = []
    for n in range(NB // 2):
        pair = [mate, c] if n == 0 else others[2 * n - 1 : 2 * n + 1]
        chip = pair[0] // 2
        row = jnp.where(lax.rem(chip, 2) == 0, pos, ROWS - 1 - pos)
        want = row * (NB * CB) + (2 * chip + lane_c) * CB + lane_1 - pos * CB
        want = jnp.where(lane_1 < ROWS * CB, want, -1)
        y = ymid.at[n % 2]
        y[0:LB, :] = mm(x, one_hot(m_id == want))
        for k in range(2):
            t = 2 * chip + k
            cols = slice(k * LANES, (k + 1) * LANES)
            y0 = y[0:SEG, cols]
            y1 = pltpu.roll(y[SEG : 2 * SEG, cols], 72, 1)
            y2 = pltpu.roll(y[2 * SEG : 3 * SEG, cols], 16, 1)
            sendbuf[t, :, 0:LANES] = jnp.where(lane_s < 72, y0, y1).astype(BF16)
            sendbuf[t, :, LANES : 2 * LANES] = jnp.where(lane_s < 16, y1, y2).astype(BF16)
        for t in pair[:1] if n == 0 else pair:
            copies.append(send(sendbuf.at[t], piece.at[c], s_send.at[t], s_recv.at[c], comp=t))
            copies[-1].start()
        if n == 0:
            m_up = send(mown, mprev, m_send.at[0], m_recv.at[0], pts=nxt)
            m_up.start()
            m_dn = send(mown, mnext, m_send.at[1], m_recv.at[1], pts=prv)
            m_dn.start()
            piece[c] = sendbuf[c]
    for get in [get_counts, get_back] + get_cells:
        get.start()

    m_up.wait()
    m_dn.wait()
    mstack[0:ROWS, :] = jnp.where(j > 0, mprev[...], 0).astype(F32)
    mstack[ROWS : 2 * ROWS, :] = mown[...].astype(F32)
    mstack[2 * ROWS : 3 * ROWS, :] = jnp.where(j < NB - 1, mnext[...], 0).astype(F32)
    g_id = iota((3 * ROWS, LANES), 0)
    l_id = iota((3 * ROWS, LANES), 1)
    rr = l_id // CB
    live = rr < ROWS + ITERS
    e_here = one_hot(jnp.logical_and(live, g_id == jnp.where(north, rr + 4, 19 - rr)))
    e_down = one_hot(jnp.logical_and(live, g_id == jnp.where(north, rr + 5, 18 - rr)))
    e_both = jnp.concatenate([e_here, e_down], axis=1)
    stack = mstack[...].astype(BF16)
    both = lax.dot_general(stack, e_both, (((0,), (0,)), ((), ())), preferred_element_type=F32)
    mexp[PAD : PAD + LON, :] = both[:, :LANES]
    mdown[...] = both[:, LANES:]
    wrap(mexp)
    ax = coef_ref[0:1, :]
    ay = coef_ref[1:2, :]
    ad = coef_ref[2:3, :]
    step_rows = 120
    for i in range(LON // step_rows):
        a = PAD + i * step_rows
        m = mexp[a : a + step_rows, :]
        lon_down = jnp.where(
            east, mexp[a + 1 : a + 1 + step_rows, :], mexp[a - 1 : a - 1 + step_rows, :]
        )
        kbuf[a : a + step_rows, :] = m * (
            1.0 - ax * lon_down - ad * mdown[i * step_rows : (i + 1) * step_rows, :]
        )
    wrap(kbuf)

    get_counts.wait()
    get_back.wait()
    width = out_ref.shape[1]
    offsets = [jnp.int32(0)]
    for i in range(NB - 1):
        offsets.append(offsets[-1] + counts[i, j])
    for a in range(0, width, SLOT_ROWS):
        size = min(SLOT_ROWS, width - a)
        picked = back[:, a : a + size]
        start = jnp.zeros_like(picked)
        place = jnp.zeros_like(picked)
        for i in range(1, NB):
            later = picked >= offsets[i]
            start = jnp.where(later, offsets[i], start)
            place = jnp.where(later, i * CAP_ROWS, place)
        within = picked - start
        place = place + within
        for g in range(1, GROUPS):
            place = place + jnp.where(within >= g * USED_ROWS, NB * CAP_ROWS - USED_ROWS, 0)
        slotv[:, a : a + size] = place
    slotv[:, width:] = jnp.zeros((1, SLOT_ROWS * SLOT_GROUPS - width), jnp.int32)
    put_slots = pltpu.make_async_copy(slotv, slots, l_sem.at[0])
    put_slots.start()
    for i, get in enumerate(get_cells):
        get.wait()
        for k in range(CAP, USED_ROWS * GROUPS):
            cells[i * CELLS + k] = 0

    src = iota((2 * LANES, LANES), 0)
    dst = iota((2 * LANES, LANES), 1)
    seg = dst // OWN
    h_pack = one_hot(
        jnp.logical_and(seg < 3, src == seg * (ROWS * CB) + (ROWS - ITERS) * CB + dst - seg * OWN)
    )
    hops = []
    for b in [c] + others:
        if hops:
            send(sendbuf.at[b], piece.at[b], s_send.at[b], s_recv.at[b], comp=b).wait_recv()
        hsend[b] = mm(piece[b], h_pack).astype(BF16)
        hops.append(send(hsend.at[b], hrecv.at[b], h_send.at[b], h_recv.at[b], pts=down))
        hops[-1].start()

    u_src = iota((2 * LANES, 3 * LANES), 0)
    u_dst = iota((2 * LANES, 3 * LANES), 1)
    u_seg = u_dst // LANES
    u_lane = u_dst - u_seg * LANES
    own_lane = jnp.logical_and(u_lane >= OWN, u_lane < OWN + ROWS * CB)
    unpack = one_hot(jnp.logical_and(own_lane, u_src == u_seg * (ROWS * CB) + u_lane - OWN))
    hu_src = iota((LANES, 3 * LANES), 0)
    hu_dst = iota((LANES, 3 * LANES), 1)
    hu_seg = hu_dst // LANES
    hu_lane = hu_dst - hu_seg * LANES
    h_unpack = one_hot(jnp.logical_and(hu_lane < OWN, hu_src == hu_seg * OWN + hu_lane))
    for hop in hops:
        hop.wait_recv()
    for b in range(NB):
        full = mm(piece[b], unpack) + mm(hrecv[b], h_unpack)
        for t in range(3):
            size = min(SEG, LB - t * SEG)
            a = PAD + b * LB + t * SEG
            va[a : a + size, :] = full[:size, t * LANES : (t + 1) * LANES] * mexp[a : a + size, :]

    wrap(va)
    wide = CHUNK + 16
    for w in (vb, vc):
        w[0:8, :] = jnp.zeros((8, LANES), F32)
        w[8 + wide : 16 + wide, :] = jnp.zeros((8, LANES), F32)
    shares = []
    for n in range(LON // CHUNK):
        first = PAD + n * CHUNK - 16
        for it in range(ITERS):
            v, w = ((va, vb), (vb, vc), (vc, vb), (vb, None))[it]
            low, size, block = (8, wide, wide // 4) if it < ITERS - 1 else (16, CHUNK, CHUNK // 6)
            for a in range(low, low + size, block):
                at = a + first if it == 0 else a
                here = v[at : at + block, :]
                side = jnp.where(east, v[at - 1 : at - 1 + block, :], v[at + 1 : at + 1 + block, :])
                new = kbuf[a + first : a + first + block, :] * here + mexp[a + first : a + first + block, :] * (
                    ax * side + ay * pltpu.roll(here, CB, 1)
                )
                if it < ITERS - 1:
                    w[a : a + block, :] = new
                else:
                    k = n * CHUNK + a - low
                    vfin[k : k + block, :] = new.astype(BF16)
        part = pl.ds(n * CHUNK, CHUNK)
        shares.append(send(vfin.at[part], vmate.at[part], v_send.at[n], v_recv.at[n], comp=mate))
        shares[-1].start()

    spreads = []
    for pair in range(ROWS // 2):
        src = iota((2 * LANES, 2 * LANES), 0)
        dst = iota((2 * LANES, 2 * LANES), 1)
        half = dst // LANES
        lane2 = dst - half * LANES
        part = lane2 - (lane2 // (2 * CB)) * (2 * CB)
        of = part // CB
        here = jnp.where(north, 2 * pair, ROWS - 1 - 2 * pair)
        then = jnp.where(north, 2 * pair + 1, ROWS - 2 - 2 * pair)
        first = OWN + jnp.where(half == 0, here, then) * CB + jnp.where(of == core, 0, LANES)
        spreads.append(
            one_hot(jnp.logical_and(lane2 < PAIR_GROUPS * 2 * CB, src == first + part - of * CB))
        )
    for n, share in enumerate(shares):
        share.wait_recv()
        part = slice(n * CHUNK, (n + 1) * CHUNK)
        values = jnp.concatenate([vfin[part, :], vmate[part, :]], axis=1)
        for pair in range(ROWS // 2):
            both = mm(values, spreads[pair])
            a = 2 * pair * LON + n * CHUNK
            tab[a : a + CHUNK, :] = both[:, :LANES]
            tab[a + LON : a + LON + CHUNK, :] = both[:, LANES:]
    c_src = iota((2 * LANES, 2 * LANES), 0)
    c_dst = iota((2 * LANES, 2 * LANES), 1)
    c_core = c_dst // LANES
    c_lane = c_dst - c_core * LANES
    c_group = c_lane // CB
    c_half = lax.rem(c_group, 2)
    c_want = c_half * LANES + (c_group // 2) * (2 * CB) + c_core * CB + c_lane - c_group * CB
    cut = one_hot(jnp.logical_and(c_group < GROUPS, c_src == c_want))
    for ref in (stage_a, stage_b):
        for half in range(2):
            ref[half, USED_ROWS:CAP_ROWS, :] = jnp.zeros((CAP_ROWS - USED_ROWS, LANES), F32)
    stride = 2 * USED_ROWS

    def block_to(d, n):
        return send(
            outgo.at[d, n], income.at[j], o_send.at[d, n], o_recv.at[j],
            comp=c - core + n, pts=d,
        )

    def gather(ref, s):
        d = lax.rem(j + 2 * lax.rem(s, NB // 2) + core, NB)
        at_d = cells.at[pl.ds(pl.multiple_of(d * CELLS, CELLS), CELLS)]
        for half in range(2):
            for r in range(USED_ROWS):
                at = at_d.at[pl.ds(half * USED_ROWS + r, (PAIR_GROUPS - 1) * stride + 1)]
                ref[half, r : r + 1, :] = merge_rows(tab, at, PAIR_GROUPS, stride, lane, 2 * CB)

    def blocks_of(ref):
        packed = jnp.concatenate([ref[0], ref[1]], axis=1)
        return mm(packed.astype(BF16), cut).astype(BF16)

    def flush(ref, s):
        d = lax.rem(j + 2 * s + core, NB)
        blocks = blocks_of(ref)
        for n in range(2):
            outgo[d, n] = blocks[:, n * LANES : (n + 1) * LANES]
            block_to(d, n).start()

    gather(stage_a, 1)

    def two_owners(q, _):
        gather(stage_b, 2 * q + 2)
        flush(stage_a, 2 * q + 1)
        gather(stage_a, 2 * q + 3)
        flush(stage_b, 2 * q + 2)
        return 0

    lax.fori_loop(0, NB // 4 - 1, two_owners, 0)
    gather(stage_b, NB // 2)
    flush(stage_a, NB // 2 - 1)
    last = lax.rem(j + core, NB)
    blocks = blocks_of(stage_b)
    outgo[last, 1] = blocks[:, LANES:]
    block_to(last, 1).start()

    @pl.when(core == 1)
    def _():
        outgo[last, 0] = blocks[:, :LANES]
        block_to(last, 0).start()

    @pl.when(core == 0)
    def _():
        income[j] = blocks[:, :LANES]

    def sent(s, _):
        d = lax.rem(j + 2 * s + core, NB)
        block_to(d, 1).wait_send()

        @pl.when(d != j)
        def _():
            block_to(d, 0).wait_send()

        return 0

    lax.fori_loop(0, NB // 2, sent, 0)

    def arrive(s, _):
        d = lax.rem(j + s, NB)

        @pl.when(jnp.logical_or(s > 0, core == 1))
        def _():
            send(
                outgo.at[d, 0], income.at[d], o_send.at[d, 0], o_recv.at[d], comp=mate, pts=d
            ).wait_recv()

        return 0

    lax.fori_loop(0, NB, arrive, 0)

    total = NB * CAP_ROWS
    got = income[...].reshape(total, LANES)
    for pair in range(GROUPS // 2):
        both = mm(got, spread_matrix(2 * pair * CB, (2 * pair + 1) * CB, SLOT_GROUPS))
        tab[2 * pair * total : (2 * pair + 1) * total, :] = both[:, :LANES]
        tab[(2 * pair + 1) * total : (2 * pair + 2) * total, :] = both[:, LANES:]
    put_slots.wait()
    slot_unroll = 32

    def slot_rows(q, _):
        for u in range(slot_unroll):
            r = q * slot_unroll + u
            at = slots.at[0, pl.ds(r, (SLOT_GROUPS - 1) * SLOT_ROWS + 1)]
            stage[pl.ds(r, 1), :] = merge_rows(tab, at, SLOT_GROUPS, SLOT_ROWS, lane)
        return 0

    lax.fori_loop(0, SLOT_ROWS // slot_unroll, slot_rows, 0)
    t_row = iota((SLOT_GROUPS * 16, LANES), 0)
    t_lane = iota((SLOT_GROUPS * 16, LANES), 1)
    group = t_row // 16
    comp = t_row - group * 16
    turn = one_hot(jnp.logical_and(comp < CB, t_lane == group * CB + comp))
    turned = lax.dot_general(
        turn, stage[...].astype(BF16), (((1,), (1,)), ((), ())), preferred_element_type=F32
    )
    for g in range(SLOT_GROUPS):
        size = min(SLOT_ROWS, width - g * SLOT_ROWS)
        out_ref[:, g * SLOT_ROWS : g * SLOT_ROWS + size] = turned[16 * g : 16 * g + CB, :size].astype(BF16)

    for copy in copies + shares:
        copy.wait_send()
    for hop in hops:
        hop.wait_send()


def whole(x, mask, coef, cells, counts, back):
    dma = pltpu.SemaphoreType.DMA
    vmem = pl.BlockSpec(memory_space=pltpu.VMEM)
    hbm = pl.BlockSpec(memory_space=pltpu.HBM)
    wrapped = PAD + LON + PAD
    chunk = CHUNK + 32
    return pl.pallas_call(
        whole_kernel,
        out_shape=jax.ShapeDtypeStruct((CB, back.shape[1]), BF16),
        in_specs=[hbm, hbm, vmem, hbm, hbm, hbm],
        out_specs=vmem,
        scratch_shapes=[
            pltpu.VMEM(x.shape, BF16),
            pltpu.VMEM((NB, SEG, 2 * LANES), BF16),
            pltpu.VMEM((NB, SEG, 2 * LANES), BF16),
            pltpu.VMEM((NB, SEG, LANES), BF16),
            pltpu.VMEM((NB, SEG, LANES), BF16),
            pltpu.VMEM((2, 3 * SEG, 2 * LANES), F32),
            pltpu.VMEM((ROWS, LON), jnp.int32),
            pltpu.VMEM((ROWS, LON), jnp.int32),
            pltpu.VMEM((ROWS, LON), jnp.int32),
            pltpu.VMEM((3 * ROWS, LON), F32),
            pltpu.VMEM((wrapped, LANES), F32),
            pltpu.VMEM((LON, LANES), F32),
            pltpu.VMEM((wrapped, LANES), F32),
            pltpu.VMEM((wrapped, LANES), F32),
            pltpu.VMEM((chunk, LANES), F32),
            pltpu.VMEM((chunk, LANES), F32),
            pltpu.VMEM((LON, LANES), BF16),
            pltpu.VMEM((LON, LANES), BF16),
            pltpu.VMEM((ROWS * LON, LANES), F32),
            pltpu.VMEM((2, CAP_ROWS, LANES), F32),
            pltpu.VMEM((2, CAP_ROWS, LANES), F32),
            pltpu.VMEM((SLOT_ROWS, LANES), F32),
            pltpu.VMEM((NB, 2, CAP_ROWS, LANES), BF16),
            pltpu.VMEM((NB, CAP_ROWS, LANES), BF16),
            pltpu.VMEM(back.shape, jnp.int32),
            pltpu.VMEM((1, SLOT_ROWS * SLOT_GROUPS), jnp.int32),
            pltpu.SMEM((NB * CELLS,), jnp.int32),
            pltpu.SMEM((NB, NB), jnp.int32),
            pltpu.SMEM((1, SLOT_ROWS * SLOT_GROUPS), jnp.int32),
            dma((NB,)), dma((NB,)), dma((NB,)), dma((NB,)), dma((2,)), dma((2,)), dma((6,)), dma((NB,)),
            dma((LON // CHUNK,)), dma((LON // CHUNK,)), dma((NB, 2)), dma((NB,)),
        ],
        compiler_params=pltpu.CompilerParams(
            collective_id=0, has_side_effects=True, vmem_limit_bytes=60 << 20
        ),
        name="propagate_and_return",
    )(x, mask, coef, cells, counts, back)


def coefficients(comp_here, pts_here):
    grid_rows = ROWS * NB
    lane = jnp.arange(LANES, dtype=jnp.int32)
    rr = lane // CB
    comp = comp_here * CB + lane % CB
    quad = comp_here % 4
    north = quad < 2
    band_row = jnp.where(north, rr - ITERS, ROWS - 1 + ITERS - rr)
    row = (pts_here * ROWS + band_row).astype(F32)

    def cosines(row_ids):
        radians = (45.0 + 0.1 * (row_ids + 0.5 - 0.5 * grid_rows)) * (math.pi / 180.0)
        return jnp.cos(radians), jnp.cos(radians + 0.05 * math.pi / 180.0)

    cos_mid, cos_upper = cosines(row)
    cos_lower = cosines(row - 1.0)[1]
    freq = (comp // ND).astype(F32)
    angle = ((comp % ND).astype(F32) + 0.5) * (2.0 * math.pi / ND)
    top = math.cos((45.0 + 0.05 * grid_rows) * math.pi / 180.0)
    speed = 0.6 * top * jnp.power(jnp.float32(1.1), -freq)
    east_x = jnp.abs(speed * jnp.cos(angle))
    north_y = jnp.abs(speed * jnp.sin(angle))
    ax = east_x / cos_mid
    up = north_y * jnp.where(north, cos_lower, cos_upper) / cos_mid
    dn = north_y * jnp.where(north, cos_upper, cos_lower) / cos_mid
    live = rr < ROWS + ITERS
    rows = [jnp.where(live, value, 0.0) for value in (ax, up, dn)]
    return jnp.stack(rows + [jnp.zeros((LANES,), F32)] * 5)


def local(spectra, land_mask, send_rows, row_counts, return_index):
    comp_here = lax.axis_index("comp")
    pts_here = lax.axis_index("pts")
    coef = coefficients(comp_here, pts_here)
    return whole(spectra, land_mask, coef, send_rows, row_counts, return_index)


def solution(mesh):
    placed = (P("comp", "pts"), P("pts", None), P("pts", None, None), P(), P("pts", None))
    return jax.shard_map(
        local, mesh=mesh, in_specs=placed, out_specs=P("comp", "pts"), check_vma=False
    )
```

```python
import functools
import math

import jax
import jax.numpy as jnp
from jax import lax
from jax.experimental import pallas as pl
from jax.experimental.pallas import tpu as pltpu
from jax.sharding import PartitionSpec as P

ND = 36
ITERS = 4
LANES = 128
CB = 9
ROWS = 8
OWN = ITERS * CB
LON = 3600
LB = 225
SEG = 80
NB = 16
PAD = 16
GROUPS = 14
CAP = 1280
CAP_ROWS = 96
USED_ROWS = 92
PAIR_GROUPS = 7
CELLS = 2048
CHUNK = 720
SLOT_ROWS = 1024
SLOT_GROUPS = 13
F32 = jnp.float32
BF16 = jnp.bfloat16


def iota(shape, dim):
    return lax.broadcasted_iota(jnp.int32, shape, dim)


def one_hot(cond):
    return jnp.where(cond, 1.0, 0.0).astype(BF16)


def mm(a, b):
    return jnp.dot(a, b, preferred_element_type=F32)


def send(src, dst, send_sem, recv_sem, **where):
    return pltpu.make_async_remote_copy(
        src_ref=src, dst_ref=dst, send_sem=send_sem, recv_sem=recv_sem,
        device_id=where, device_id_type=pl.DeviceIdType.MESH,
    )


def merge_rows(tab, at, groups, stride, lane, width=CB):
    row = tab[pl.ds(at[0], 1), :]
    for g in range(1, groups):
        row = jnp.where(lane >= width * g, tab[pl.ds(at[g * stride], 1), :], row)
    return row


def spread_matrix(first, second, live):
    src = iota((LANES, 2 * LANES), 0)
    dst = iota((LANES, 2 * LANES), 1)
    half = dst // LANES
    lane2 = dst - half * LANES
    return one_hot(
        jnp.logical_and(lane2 < live * CB, src == jnp.where(half == 0, first, second) + lane2 - (lane2 // CB) * CB)
    )


def wrap(ref):
    ref[0:PAD, :] = ref[LON : LON + PAD, :]
    ref[PAD + LON : 2 * PAD + LON, :] = ref[PAD : 2 * PAD, :]


def partners(c):
    z = c // 2
    order = [z * 2 + 1 - (c - z * 2)]
    for dist in (1, 2, 3, 4):
        for chip in (4,) if dist == 4 else (dist, 8 - dist):
            for core in range(2):
                order.append(lax.rem(z + chip, 8) * 2 + core)
    return order


def whole_kernel(
    x_ref, mask_ref, coef_ref, cell_ref, count_ref, back_ref, out_ref,
    xin, sendbuf, piece, hsend, hrecv, ymid, mprev, mown, mnext, mstack, mexp, mdown, kbuf, va, vb, vc,
    vfin, vmate, tab, stage, outgo, income, back, slotv, cells, counts, slots,
    s_send, s_recv, h_send, h_recv, m_send, m_recv, l_sem, c_sem, v_send, v_recv, o_send, o_recv,
):
    c = lax.axis_index("comp")
    j = lax.axis_index("pts")
    nxt = lax.rem(j + 1, NB)
    prv = lax.rem(j + NB - 1, NB)
    quad = lax.rem(c, 4)
    north = quad < 2
    east = jnp.logical_or(quad == 0, quad == 3)
    down = jnp.where(north, nxt, prv)
    others = partners(c)
    core = lax.rem(c, 2)
    mate = c + 1 - 2 * core

    get_x = pltpu.make_async_copy(x_ref, xin, l_sem.at[1])
    get_mask = pltpu.make_async_copy(mask_ref, mown, l_sem.at[2])
    get_x.start()
    get_mask.start()

    barrier = pltpu.get_barrier_semaphore()

    def greet(**where):
        pl.semaphore_signal(barrier, inc=1, device_id=where, device_id_type=pl.DeviceIdType.MESH)

    for other in others:
        greet(comp=other)
    greet(pts=nxt)
    greet(pts=prv)
    for s in range(1, NB):
        greet(comp=c - core + s % 2, pts=lax.rem(j + NB - s, NB))
    get_counts = pltpu.make_async_copy(count_ref, counts, l_sem.at[3])
    get_back = pltpu.make_async_copy(back_ref, back, l_sem.at[4])
    get_cells = [
        pltpu.make_async_copy(cell_ref.at[0, i], cells.at[pl.ds(i * CELLS, CAP)], c_sem.at[i]) for i in range(NB)
    ]
    for n in range(2):
        ymid[n, LB : 3 * SEG, :] = jnp.zeros((3 * SEG - LB, 2 * LANES), F32)
    get_x.wait()
    get_mask.wait()
    pl.semaphore_wait(barrier, NB + 1 + NB - 2 + 2 * core)

    m_id = iota((ROWS * NB * CB, 2 * LANES), 0)
    lane = iota((1, LANES), 1)
    lane_2 = iota((1, 2 * LANES), 1)
    lane_c = lane_2 // LANES
    lane_1 = lane_2 - lane_c * LANES
    pos = lane_1 // CB
    lane_s = iota((SEG, LANES), 1)
    x = xin[...]
    copies = []
    for n in range(NB // 2):
        pair = [mate, c] if n == 0 else others[2 * n - 1 : 2 * n + 1]
        chip = pair[0] // 2
        row = jnp.where(lax.rem(chip, 2) == 0, pos, ROWS - 1 - pos)
        want = row * (NB * CB) + (2 * chip + lane_c) * CB + lane_1 - pos * CB
        want = jnp.where(lane_1 < ROWS * CB, want, -1)
        y = ymid.at[n % 2]
        y[0:LB, :] = mm(x, one_hot(m_id == want))
        for k in range(2):
            t = 2 * chip + k
            cols = slice(k * LANES, (k + 1) * LANES)
            y0 = y[0:SEG, cols]
            y1 = pltpu.roll(y[SEG : 2 * SEG, cols], 72, 1)
            y2 = pltpu.roll(y[2 * SEG : 3 * SEG, cols], 16, 1)
            sendbuf[t, :, 0:LANES] = jnp.where(lane_s < 72, y0, y1).astype(BF16)
            sendbuf[t, :, LANES : 2 * LANES] = jnp.where(lane_s < 16, y1, y2).astype(BF16)
        for t in pair[:1] if n == 0 else pair:
            copies.append(send(sendbuf.at[t], piece.at[c], s_send.at[t], s_recv.at[c], comp=t))
            copies[-1].start()
        if n == 0:
            m_up = send(mown, mprev, m_send.at[0], m_recv.at[0], pts=nxt)
            m_up.start()
            m_dn = send(mown, mnext, m_send.at[1], m_recv.at[1], pts=prv)
            m_dn.start()
            piece[c] = sendbuf[c]
    for get in [get_counts, get_back] + get_cells:
        get.start()

    m_up.wait()
    m_dn.wait()
    mstack[0:ROWS, :] = jnp.where(j > 0, mprev[...], 0).astype(F32)
    mstack[ROWS : 2 * ROWS, :] = mown[...].astype(F32)
    mstack[2 * ROWS : 3 * ROWS, :] = jnp.where(j < NB - 1, mnext[...], 0).astype(F32)
    g_id = iota((3 * ROWS, LANES), 0)
    l_id = iota((3 * ROWS, LANES), 1)
    rr = l_id // CB
    live = rr < ROWS + ITERS
    e_here = one_hot(jnp.logical_and(live, g_id == jnp.where(north, rr + 4, 19 - rr)))
    e_down = one_hot(jnp.logical_and(live, g_id == jnp.where(north, rr + 5, 18 - rr)))
    e_both = jnp.concatenate([e_here, e_down], axis=1)
    stack = mstack[...].astype(BF16)
    both = lax.dot_general(stack, e_both, (((0,), (0,)), ((), ())), preferred_element_type=F32)
    mexp[PAD : PAD + LON, :] = both[:, :LANES]
    mdown[...] = both[:, LANES:]
    wrap(mexp)
    ax = coef_ref[0:1, :]
    ay = coef_ref[1:2, :]
    ad = coef_ref[2:3, :]
    step_rows = 120
    for i in range(LON // step_rows):
        a = PAD + i * step_rows
        m = mexp[a : a + step_rows, :]
        lon_down = jnp.where(
            east, mexp[a + 1 : a + 1 + step_rows, :], mexp[a - 1 : a - 1 + step_rows, :]
        )
        kbuf[a : a + step_rows, :] = m * (
            1.0 - ax * lon_down - ad * mdown[i * step_rows : (i + 1) * step_rows, :]
        )
    wrap(kbuf)

    get_counts.wait()
    get_back.wait()
    width = out_ref.shape[1]
    offsets = [jnp.int32(0)]
    for i in range(NB - 1):
        offsets.append(offsets[-1] + counts[i, j])
    for a in range(0, width, SLOT_ROWS):
        size = min(SLOT_ROWS, width - a)
        picked = back[:, a : a + size]
        start = jnp.zeros_like(picked)
        place = jnp.zeros_like(picked)
        for i in range(1, NB):
            later = picked >= offsets[i]
            start = jnp.where(later, offsets[i], start)
            place = jnp.where(later, i * CAP_ROWS, place)
        within = picked - start
        place = place + within
        for g in range(1, GROUPS):
            place = place + jnp.where(within >= g * USED_ROWS, NB * CAP_ROWS - USED_ROWS, 0)
        slotv[:, a : a + size] = place
    slotv[:, width:] = jnp.zeros((1, SLOT_ROWS * SLOT_GROUPS - width), jnp.int32)
    put_slots = pltpu.make_async_copy(slotv, slots, l_sem.at[0])
    put_slots.start()
    for i, get in enumerate(get_cells):
        get.wait()
        for k in range(CAP, USED_ROWS * GROUPS):
            cells[i * CELLS + k] = 0

    src = iota((2 * LANES, LANES), 0)
    dst = iota((2 * LANES, LANES), 1)
    seg = dst // OWN
    h_pack = one_hot(
        jnp.logical_and(seg < 3, src == seg * (ROWS * CB) + (ROWS - ITERS) * CB + dst - seg * OWN)
    )
    hops = []
    for b in [c] + others:
        if hops:
            send(sendbuf.at[b], piece.at[b], s_send.at[b], s_recv.at[b], comp=b).wait_recv()
        hsend[b] = mm(piece[b], h_pack).astype(BF16)
        hops.append(send(hsend.at[b], hrecv.at[b], h_send.at[b], h_recv.at[b], pts=down))
        hops[-1].start()

    u_src = iota((2 * LANES, 3 * LANES), 0)
    u_dst = iota((2 * LANES, 3 * LANES), 1)
    u_seg = u_dst // LANES
    u_lane = u_dst - u_seg * LANES
    own_lane = jnp.logical_and(u_lane >= OWN, u_lane < OWN + ROWS * CB)
    unpack = one_hot(jnp.logical_and(own_lane, u_src == u_seg * (ROWS * CB) + u_lane - OWN))
    hu_src = iota((LANES, 3 * LANES), 0)
    hu_dst = iota((LANES, 3 * LANES), 1)
    hu_seg = hu_dst // LANES
    hu_lane = hu_dst - hu_seg * LANES
    h_unpack = one_hot(jnp.logical_and(hu_lane < OWN, hu_src == hu_seg * OWN + hu_lane))
    for hop in hops:
        hop.wait_recv()
    for b in range(NB):
        full = mm(piece[b], unpack) + mm(hrecv[b], h_unpack)
        for t in range(3):
            size = min(SEG, LB - t * SEG)
            a = PAD + b * LB + t * SEG
            va[a : a + size, :] = full[:size, t * LANES : (t + 1) * LANES] * mexp[a : a + size, :]

    wrap(va)
    wide = CHUNK + 16
    for w in (vb, vc):
        w[0:8, :] = jnp.zeros((8, LANES), F32)
        w[8 + wide : 16 + wide, :] = jnp.zeros((8, LANES), F32)
    shares = []
    for n in range(LON // CHUNK):
        first = PAD + n * CHUNK - 16
        for it in range(ITERS):
            v, w = ((va, vb), (vb, vc), (vc, vb), (vb, None))[it]
            low, size, block = (8, wide, wide // 4) if it < ITERS - 1 else (16, CHUNK, CHUNK // 6)
            for a in range(low, low + size, block):
                at = a + first if it == 0 else a
                here = v[at : at + block, :]
                side = jnp.where(east, v[at - 1 : at - 1 + block, :], v[at + 1 : at + 1 + block, :])
                new = kbuf[a + first : a + first + block, :] * here + mexp[a + first : a + first + block, :] * (
                    ax * side + ay * pltpu.roll(here, CB, 1)
                )
                if it < ITERS - 1:
                    w[a : a + block, :] = new
                else:
                    k = n * CHUNK + a - low
                    vfin[k : k + block, :] = new.astype(BF16)
        part = pl.ds(n * CHUNK, CHUNK)
        shares.append(send(vfin.at[part], vmate.at[part], v_send.at[n], v_recv.at[n], comp=mate))
        shares[-1].start()

    spreads = []
    for pair in range(ROWS // 2):
        src = iota((2 * LANES, 2 * LANES), 0)
        dst = iota((2 * LANES, 2 * LANES), 1)
        half = dst // LANES
        lane2 = dst - half * LANES
        part = lane2 - (lane2 // (2 * CB)) * (2 * CB)
        of = part // CB
        here = jnp.where(north, 2 * pair, ROWS - 1 - 2 * pair)
        then = jnp.where(north, 2 * pair + 1, ROWS - 2 - 2 * pair)
        first = OWN + jnp.where(half == 0, here, then) * CB + jnp.where(of == core, 0, LANES)
        spreads.append(
            one_hot(jnp.logical_and(lane2 < PAIR_GROUPS * 2 * CB, src == first + part - of * CB))
        )
    for n, share in enumerate(shares):
        share.wait_recv()
        part = slice(n * CHUNK, (n + 1) * CHUNK)
        values = jnp.concatenate([vfin[part, :], vmate[part, :]], axis=1)
        for pair in range(ROWS // 2):
            both = mm(values, spreads[pair])
            a = 2 * pair * LON + n * CHUNK
            tab[a : a + CHUNK, :] = both[:, :LANES]
            tab[a + LON : a + LON + CHUNK, :] = both[:, LANES:]
    c_src = iota((2 * LANES, 2 * LANES), 0)
    c_dst = iota((2 * LANES, 2 * LANES), 1)
    c_core = c_dst // LANES
    c_lane = c_dst - c_core * LANES
    c_group = c_lane // CB
    c_half = lax.rem(c_group, 2)
    c_want = c_half * LANES + (c_group // 2) * (2 * CB) + c_core * CB + c_lane - c_group * CB
    cut = one_hot(jnp.logical_and(c_group < GROUPS, c_src == c_want))
    for half in range(2):
        a = half * CAP_ROWS + USED_ROWS
        stage[a : a + CAP_ROWS - USED_ROWS, :] = jnp.zeros((CAP_ROWS - USED_ROWS, LANES), F32)
    stride = 2 * USED_ROWS
    unroll = USED_ROWS // 2

    def block_to(d, n):
        return send(
            outgo.at[d, n], income.at[j], o_send.at[d, n], o_recv.at[j],
            comp=c - core + n, pts=d,
        )

    def gather(d):
        def rows(q, _):
            base = d * CELLS + q * unroll
            to = q * unroll + (q // 2) * (CAP_ROWS - USED_ROWS)
            for u in range(unroll):
                at = cells.at[pl.ds(base + u, (PAIR_GROUPS - 1) * stride + 1)]
                stage[pl.ds(to + u, 1), :] = merge_rows(tab, at, PAIR_GROUPS, stride, lane, 2 * CB)
            return 0

        lax.fori_loop(0, 4, rows, 0)
        packed = jnp.concatenate([stage[0:CAP_ROWS, :], stage[CAP_ROWS : 2 * CAP_ROWS, :]], axis=1)
        return mm(packed.astype(BF16), cut).astype(BF16)

    def owner(s, _):
        d = lax.rem(j + 2 * s + core, NB)
        blocks = gather(d)
        for n in range(2):
            outgo[d, n] = blocks[:, n * LANES : (n + 1) * LANES]
            block_to(d, n).start()
        return 0

    lax.fori_loop(1, NB // 2, owner, 0)
    last = lax.rem(j + core, NB)
    blocks = gather(last)
    outgo[last, 1] = blocks[:, LANES:]
    block_to(last, 1).start()

    @pl.when(core == 1)
    def _():
        outgo[last, 0] = blocks[:, :LANES]
        block_to(last, 0).start()

    @pl.when(core == 0)
    def _():
        income[j] = blocks[:, :LANES]

    def sent(s, _):
        d = lax.rem(j + 2 * s + core, NB)
        block_to(d, 1).wait_send()

        @pl.when(d != j)
        def _():
            block_to(d, 0).wait_send()

        return 0

    lax.fori_loop(0, NB // 2, sent, 0)

    def arrive(s, _):
        d = lax.rem(j + s, NB)

        @pl.when(jnp.logical_or(s > 0, core == 1))
        def _():
            send(
                outgo.at[d, 0], income.at[d], o_send.at[d, 0], o_recv.at[d], comp=mate, pts=d
            ).wait_recv()

        return 0

    lax.fori_loop(0, NB, arrive, 0)

    total = NB * CAP_ROWS
    got = income[...].reshape(total, LANES)
    for pair in range(GROUPS // 2):
        both = mm(got, spread_matrix(2 * pair * CB, (2 * pair + 1) * CB, SLOT_GROUPS))
        tab[2 * pair * total : (2 * pair + 1) * total, :] = both[:, :LANES]
        tab[(2 * pair + 1) * total : (2 * pair + 2) * total, :] = both[:, LANES:]
    put_slots.wait()
    slot_unroll = 32

    def slot_rows(q, _):
        for u in range(slot_unroll):
            r = q * slot_unroll + u
            at = slots.at[0, pl.ds(r, (SLOT_GROUPS - 1) * SLOT_ROWS + 1)]
            stage[pl.ds(r, 1), :] = merge_rows(tab, at, SLOT_GROUPS, SLOT_ROWS, lane)
        return 0

    lax.fori_loop(0, SLOT_ROWS // slot_unroll, slot_rows, 0)
    t_row = iota((SLOT_GROUPS * 16, LANES), 0)
    t_lane = iota((SLOT_GROUPS * 16, LANES), 1)
    group = t_row // 16
    comp = t_row - group * 16
    turn = one_hot(jnp.logical_and(comp < CB, t_lane == group * CB + comp))
    turned = lax.dot_general(
        turn, stage[...].astype(BF16), (((1,), (1,)), ((), ())), preferred_element_type=F32
    )
    for g in range(SLOT_GROUPS):
        size = min(SLOT_ROWS, width - g * SLOT_ROWS)
        out_ref[:, g * SLOT_ROWS : g * SLOT_ROWS + size] = turned[16 * g : 16 * g + CB, :size].astype(BF16)

    for copy in copies + shares:
        copy.wait_send()
    for hop in hops:
        hop.wait_send()


def whole(x, mask, coef, cells, counts, back):
    dma = pltpu.SemaphoreType.DMA
    vmem = pl.BlockSpec(memory_space=pltpu.VMEM)
    hbm = pl.BlockSpec(memory_space=pltpu.HBM)
    wrapped = PAD + LON + PAD
    chunk = CHUNK + 32
    return pl.pallas_call(
        whole_kernel,
        out_shape=jax.ShapeDtypeStruct((CB, back.shape[1]), BF16),
        in_specs=[hbm, hbm, vmem, hbm, hbm, hbm],
        out_specs=vmem,
        scratch_shapes=[
            pltpu.VMEM(x.shape, BF16),
            pltpu.VMEM((NB, SEG, 2 * LANES), BF16),
            pltpu.VMEM((NB, SEG, 2 * LANES), BF16),
            pltpu.VMEM((NB, SEG, LANES), BF16),
            pltpu.VMEM((NB, SEG, LANES), BF16),
            pltpu.VMEM((2, 3 * SEG, 2 * LANES), F32),
            pltpu.VMEM((ROWS, LON), jnp.int32),
            pltpu.VMEM((ROWS, LON), jnp.int32),
            pltpu.VMEM((ROWS, LON), jnp.int32),
            pltpu.VMEM((3 * ROWS, LON), F32),
            pltpu.VMEM((wrapped, LANES), F32),
            pltpu.VMEM((LON, LANES), F32),
            pltpu.VMEM((wrapped, LANES), F32),
            pltpu.VMEM((wrapped, LANES), F32),
            pltpu.VMEM((chunk, LANES), F32),
            pltpu.VMEM((chunk, LANES), F32),
            pltpu.VMEM((LON, LANES), BF16),
            pltpu.VMEM((LON, LANES), BF16),
            pltpu.VMEM((ROWS * LON, LANES), F32),
            pltpu.VMEM((SLOT_ROWS, LANES), F32),
            pltpu.VMEM((NB, 2, CAP_ROWS, LANES), BF16),
            pltpu.VMEM((NB, CAP_ROWS, LANES), BF16),
            pltpu.VMEM(back.shape, jnp.int32),
            pltpu.VMEM((1, SLOT_ROWS * SLOT_GROUPS), jnp.int32),
            pltpu.SMEM((NB * CELLS,), jnp.int32),
            pltpu.SMEM((NB, NB), jnp.int32),
            pltpu.SMEM((1, SLOT_ROWS * SLOT_GROUPS), jnp.int32),
            dma((NB,)), dma((NB,)), dma((NB,)), dma((NB,)), dma((2,)), dma((2,)), dma((6,)), dma((NB,)),
            dma((LON // CHUNK,)), dma((LON // CHUNK,)), dma((NB, 2)), dma((NB,)),
        ],
        compiler_params=pltpu.CompilerParams(
            collective_id=0, has_side_effects=True, vmem_limit_bytes=60 << 20
        ),
        name="propagate_and_return",
    )(x, mask, coef, cells, counts, back)


def coefficients(comp_here, pts_here):
    grid_rows = ROWS * NB
    lane = jnp.arange(LANES, dtype=jnp.int32)
    rr = lane // CB
    comp = comp_here * CB + lane % CB
    quad = comp_here % 4
    north = quad < 2
    band_row = jnp.where(north, rr - ITERS, ROWS - 1 + ITERS - rr)
    row = (pts_here * ROWS + band_row).astype(F32)

    def cosines(row_ids):
        radians = (45.0 + 0.1 * (row_ids + 0.5 - 0.5 * grid_rows)) * (math.pi / 180.0)
        return jnp.cos(radians), jnp.cos(radians + 0.05 * math.pi / 180.0)

    cos_mid, cos_upper = cosines(row)
    cos_lower = cosines(row - 1.0)[1]
    freq = (comp // ND).astype(F32)
    angle = ((comp % ND).astype(F32) + 0.5) * (2.0 * math.pi / ND)
    top = math.cos((45.0 + 0.05 * grid_rows) * math.pi / 180.0)
    speed = 0.6 * top * jnp.power(jnp.float32(1.1), -freq)
    east_x = jnp.abs(speed * jnp.cos(angle))
    north_y = jnp.abs(speed * jnp.sin(angle))
    ax = east_x / cos_mid
    up = north_y * jnp.where(north, cos_lower, cos_upper) / cos_mid
    dn = north_y * jnp.where(north, cos_upper, cos_lower) / cos_mid
    live = rr < ROWS + ITERS
    rows = [jnp.where(live, value, 0.0) for value in (ax, up, dn)]
    return jnp.stack(rows + [jnp.zeros((LANES,), F32)] * 5)


def local(spectra, land_mask, send_rows, row_counts, return_index):
    comp_here = lax.axis_index("comp")
    pts_here = lax.axis_index("pts")
    coef = coefficients(comp_here, pts_here)
    return whole(spectra, land_mask, coef, send_rows, row_counts, return_index)


def solution(mesh):
    placed = (P("comp", "pts"), P("pts", None), P("pts", None, None), P(), P("pts", None))
    return jax.shard_map(
        local, mesh=mesh, in_specs=placed, out_specs=P("comp", "pts"), check_vma=False
    )
```

```python
import functools
import math

import jax
import jax.numpy as jnp
from jax import lax
from jax.experimental import pallas as pl
from jax.experimental.pallas import tpu as pltpu
from jax.sharding import PartitionSpec as P

ND = 36
ITERS = 4
LANES = 128
CB = 9
ROWS = 8
OWN = ITERS * CB
LON = 3600
LB = 225
SEG = 80
NB = 16
PAD = 16
GROUPS = 14
CAP = 1280
CAP_ROWS = 96
USED_ROWS = 92
PAIR_GROUPS = 7
CELLS = 2048
CHUNK = 720
SLOT_ROWS = 1024
SLOT_GROUPS = 13
F32 = jnp.float32
BF16 = jnp.bfloat16


def iota(shape, dim):
    return lax.broadcasted_iota(jnp.int32, shape, dim)


def one_hot(cond):
    return jnp.where(cond, 1.0, 0.0).astype(BF16)


def mm(a, b):
    return jnp.dot(a, b, preferred_element_type=F32)


def send(src, dst, send_sem, recv_sem, **where):
    return pltpu.make_async_remote_copy(
        src_ref=src, dst_ref=dst, send_sem=send_sem, recv_sem=recv_sem,
        device_id=where, device_id_type=pl.DeviceIdType.MESH,
    )


def merge_rows(tab, at, groups, stride, lane, width=CB):
    row = tab[pl.ds(at[0], 1), :]
    for g in range(1, groups):
        row = jnp.where(lane >= width * g, tab[pl.ds(at[g * stride], 1), :], row)
    return row


def spread_matrix(first, second, live):
    src = iota((LANES, 2 * LANES), 0)
    dst = iota((LANES, 2 * LANES), 1)
    half = dst // LANES
    lane2 = dst - half * LANES
    return one_hot(
        jnp.logical_and(lane2 < live * CB, src == jnp.where(half == 0, first, second) + lane2 - (lane2 // CB) * CB)
    )


def wrap(ref):
    ref[0:PAD, :] = ref[LON : LON + PAD, :]
    ref[PAD + LON : 2 * PAD + LON, :] = ref[PAD : 2 * PAD, :]


def partners(c):
    z = c // 2
    order = [z * 2 + 1 - (c - z * 2)]
    for dist in (1, 2, 3, 4):
        for chip in (4,) if dist == 4 else (dist, 8 - dist):
            for core in range(2):
                order.append(lax.rem(z + chip, 8) * 2 + core)
    return order


def whole_kernel(
    x_ref, mask_ref, coef_ref, cell_ref, count_ref, back_ref, out_ref,
    xin, sendbuf, piece, hsend, hrecv, ymid, mprev, mown, mnext, mstack, mexp, mdown, kbuf, va, vb, vc,
    vfin, vmate, tab, stage, outgo, income, back, slotv, cells, counts, slots,
    s_send, s_recv, h_send, h_recv, m_send, m_recv, l_sem, c_sem, v_send, v_recv, o_send, o_recv,
):
    c = lax.axis_index("comp")
    j = lax.axis_index("pts")
    nxt = lax.rem(j + 1, NB)
    prv = lax.rem(j + NB - 1, NB)
    quad = lax.rem(c, 4)
    north = quad < 2
    east = jnp.logical_or(quad == 0, quad == 3)
    down = jnp.where(north, nxt, prv)
    others = partners(c)
    core = lax.rem(c, 2)
    mate = c + 1 - 2 * core

    get_x = pltpu.make_async_copy(x_ref, xin, l_sem.at[1])
    get_mask = pltpu.make_async_copy(mask_ref, mown, l_sem.at[2])
    get_x.start()
    get_mask.start()

    barrier = pltpu.get_barrier_semaphore()

    def greet(**where):
        pl.semaphore_signal(barrier, inc=1, device_id=where, device_id_type=pl.DeviceIdType.MESH)

    for other in others:
        greet(comp=other)
    greet(pts=nxt)
    greet(pts=prv)
    for s in range(1, NB):
        greet(comp=c - core + s % 2, pts=lax.rem(j + NB - s, NB))
    get_counts = pltpu.make_async_copy(count_ref, counts, l_sem.at[3])
    get_back = pltpu.make_async_copy(back_ref, back, l_sem.at[4])
    get_cells = [
        pltpu.make_async_copy(cell_ref.at[0, i], cells.at[pl.ds(i * CELLS, CAP)], c_sem.at[i]) for i in range(NB)
    ]
    for n in range(2):
        ymid[n, LB : 3 * SEG, :] = jnp.zeros((3 * SEG - LB, 2 * LANES), F32)
    get_x.wait()
    get_mask.wait()
    pl.semaphore_wait(barrier, NB + 1 + NB - 2 + 2 * core)

    m_id = iota((ROWS * NB * CB, 2 * LANES), 0)
    lane = iota((1, LANES), 1)
    lane_2 = iota((1, 2 * LANES), 1)
    lane_c = lane_2 // LANES
    lane_1 = lane_2 - lane_c * LANES
    pos = lane_1 // CB
    lane_s = iota((SEG, LANES), 1)
    x = xin[...]
    copies = []
    for n in range(NB // 2):
        pair = [mate, c] if n == 0 else others[2 * n - 1 : 2 * n + 1]
        chip = pair[0] // 2
        row = jnp.where(lax.rem(chip, 2) == 0, pos, ROWS - 1 - pos)
        want = row * (NB * CB) + (2 * chip + lane_c) * CB + lane_1 - pos * CB
        want = jnp.where(lane_1 < ROWS * CB, want, -1)
        y = ymid.at[n % 2]
        y[0:LB, :] = mm(x, one_hot(m_id == want))
        for k in range(2):
            t = 2 * chip + k
            cols = slice(k * LANES, (k + 1) * LANES)
            y0 = y[0:SEG, cols]
            y1 = pltpu.roll(y[SEG : 2 * SEG, cols], 72, 1)
            y2 = pltpu.roll(y[2 * SEG : 3 * SEG, cols], 16, 1)
            sendbuf[t, :, 0:LANES] = jnp.where(lane_s < 72, y0, y1).astype(BF16)
            sendbuf[t, :, LANES : 2 * LANES] = jnp.where(lane_s < 16, y1, y2).astype(BF16)
        for t in pair[:1] if n == 0 else pair:
            copies.append(send(sendbuf.at[t], piece.at[c], s_send.at[t], s_recv.at[c], comp=t))
            copies[-1].start()
        if n == 0:
            m_up = send(mown, mprev, m_send.at[0], m_recv.at[0], pts=nxt)
            m_up.start()
            m_dn = send(mown, mnext, m_send.at[1], m_recv.at[1], pts=prv)
            m_dn.start()
            piece[c] = sendbuf[c]
    for get in [get_counts, get_back] + get_cells:
        get.start()

    m_up.wait()
    m_dn.wait()
    mstack[0:ROWS, :] = jnp.where(j > 0, mprev[...], 0).astype(F32)
    mstack[ROWS : 2 * ROWS, :] = mown[...].astype(F32)
    mstack[2 * ROWS : 3 * ROWS, :] = jnp.where(j < NB - 1, mnext[...], 0).astype(F32)
    g_id = iota((3 * ROWS, LANES), 0)
    l_id = iota((3 * ROWS, LANES), 1)
    rr = l_id // CB
    live = rr < ROWS + ITERS
    e_here = one_hot(jnp.logical_and(live, g_id == jnp.where(north, rr + 4, 19 - rr)))
    e_down = one_hot(jnp.logical_and(live, g_id == jnp.where(north, rr + 5, 18 - rr)))
    e_both = jnp.concatenate([e_here, e_down], axis=1)
    stack = mstack[...].astype(BF16)
    both = lax.dot_general(stack, e_both, (((0,), (0,)), ((), ())), preferred_element_type=F32)
    mexp[PAD : PAD + LON, :] = both[:, :LANES]
    mdown[...] = both[:, LANES:]
    wrap(mexp)
    ax = coef_ref[0:1, :]
    ay = coef_ref[1:2, :]
    ad = coef_ref[2:3, :]
    step_rows = 120
    for i in range(LON // step_rows):
        a = PAD + i * step_rows
        m = mexp[a : a + step_rows, :]
        lon_down = jnp.where(
            east, mexp[a + 1 : a + 1 + step_rows, :], mexp[a - 1 : a - 1 + step_rows, :]
        )
        kbuf[a : a + step_rows, :] = m * (
            1.0 - ax * lon_down - ad * mdown[i * step_rows : (i + 1) * step_rows, :]
        )
    wrap(kbuf)

    get_counts.wait()
    get_back.wait()
    width = out_ref.shape[1]
    offsets = [jnp.int32(0)]
    for i in range(NB - 1):
        offsets.append(offsets[-1] + counts[i, j])
    for a in range(0, width, SLOT_ROWS):
        size = min(SLOT_ROWS, width - a)
        picked = back[:, a : a + size]
        start = jnp.zeros_like(picked)
        place = jnp.zeros_like(picked)
        for i in range(1, NB):
            later = picked >= offsets[i]
            start = jnp.where(later, offsets[i], start)
            place = jnp.where(later, i * CAP_ROWS, place)
        within = picked - start
        place = place + within
        for g in range(1, GROUPS):
            place = place + jnp.where(within >= g * USED_ROWS, NB * CAP_ROWS - USED_ROWS, 0)
        slotv[:, a : a + size] = place
    slotv[:, width:] = jnp.zeros((1, SLOT_ROWS * SLOT_GROUPS - width), jnp.int32)
    put_slots = pltpu.make_async_copy(slotv, slots, l_sem.at[0])
    put_slots.start()
    for i, get in enumerate(get_cells):
        get.wait()
        for k in range(CAP, USED_ROWS * GROUPS):
            cells[i * CELLS + k] = 0

    src = iota((2 * LANES, LANES), 0)
    dst = iota((2 * LANES, LANES), 1)
    seg = dst // OWN
    h_pack = one_hot(
        jnp.logical_and(seg < 3, src == seg * (ROWS * CB) + (ROWS - ITERS) * CB + dst - seg * OWN)
    )
    hops = []
    for b in [c] + others:
        if hops:
            send(sendbuf.at[b], piece.at[b], s_send.at[b], s_recv.at[b], comp=b).wait_recv()
        hsend[b] = mm(piece[b], h_pack).astype(BF16)
        hops.append(send(hsend.at[b], hrecv.at[b], h_send.at[b], h_recv.at[b], pts=down))
        hops[-1].start()

    u_src = iota((2 * LANES, 3 * LANES), 0)
    u_dst = iota((2 * LANES, 3 * LANES), 1)
    u_seg = u_dst // LANES
    u_lane = u_dst - u_seg * LANES
    own_lane = jnp.logical_and(u_lane >= OWN, u_lane < OWN + ROWS * CB)
    unpack = one_hot(jnp.logical_and(own_lane, u_src == u_seg * (ROWS * CB) + u_lane - OWN))
    hu_src = iota((LANES, 3 * LANES), 0)
    hu_dst = iota((LANES, 3 * LANES), 1)
    hu_seg = hu_dst // LANES
    hu_lane = hu_dst - hu_seg * LANES
    h_unpack = one_hot(jnp.logical_and(hu_lane < OWN, hu_src == hu_seg * OWN + hu_lane))
    for hop in hops:
        hop.wait_recv()
    for b in range(NB):
        full = mm(piece[b], unpack) + mm(hrecv[b], h_unpack)
        for t in range(3):
            size = min(SEG, LB - t * SEG)
            a = PAD + b * LB + t * SEG
            va[a : a + size, :] = full[:size, t * LANES : (t + 1) * LANES] * mexp[a : a + size, :]

    wrap(va)
    wide = CHUNK + 16
    for w in (vb, vc):
        w[0:8, :] = jnp.zeros((8, LANES), F32)
        w[8 + wide : 16 + wide, :] = jnp.zeros((8, LANES), F32)
    shares = []
    for n in range(LON // CHUNK):
        first = PAD + n * CHUNK - 16
        for it in range(ITERS):
            v, w = ((va, vb), (vb, vc), (vc, vb), (vb, None))[it]
            low, size, block = (8, wide, wide // 4) if it < ITERS - 1 else (16, CHUNK, CHUNK // 6)
            for a in range(low, low + size, block):
                at = a + first if it == 0 else a
                here = v[at : at + block, :]
                side = jnp.where(east, v[at - 1 : at - 1 + block, :], v[at + 1 : at + 1 + block, :])
                new = kbuf[a + first : a + first + block, :] * here + mexp[a + first : a + first + block, :] * (
                    ax * side + ay * pltpu.roll(here, CB, 1)
                )
                if it < ITERS - 1:
                    w[a : a + block, :] = new
                else:
                    k = n * CHUNK + a - low
                    vfin[k : k + block, :] = new.astype(BF16)
        part = pl.ds(n * CHUNK, CHUNK)
        shares.append(send(vfin.at[part], vmate.at[part], v_send.at[n], v_recv.at[n], comp=mate))
        shares[-1].start()

    spreads = []
    for pair in range(ROWS // 2):
        src = iota((2 * LANES, 2 * LANES), 0)
        dst = iota((2 * LANES, 2 * LANES), 1)
        half = dst // LANES
        lane2 = dst - half * LANES
        part = lane2 - (lane2 // (2 * CB)) * (2 * CB)
        of = part // CB
        here = jnp.where(north, 2 * pair, ROWS - 1 - 2 * pair)
        then = jnp.where(north, 2 * pair + 1, ROWS - 2 - 2 * pair)
        first = OWN + jnp.where(half == 0, here, then) * CB + jnp.where(of == core, 0, LANES)
        spreads.append(
            one_hot(jnp.logical_and(lane2 < PAIR_GROUPS * 2 * CB, src == first + part - of * CB))
        )
    for n, share in enumerate(shares):
        share.wait_recv()
        part = slice(n * CHUNK, (n + 1) * CHUNK)
        values = jnp.concatenate([vfin[part, :], vmate[part, :]], axis=1)
        for pair in range(ROWS // 2):
            both = mm(values, spreads[pair])
            a = 2 * pair * LON + n * CHUNK
            tab[a : a + CHUNK, :] = both[:, :LANES]
            tab[a + LON : a + LON + CHUNK, :] = both[:, LANES:]
    c_src = iota((2 * LANES, 2 * LANES), 0)
    c_dst = iota((2 * LANES, 2 * LANES), 1)
    c_core = c_dst // LANES
    c_lane = c_dst - c_core * LANES
    c_group = c_lane // CB
    c_half = lax.rem(c_group, 2)
    c_want = c_half * LANES + (c_group // 2) * (2 * CB) + c_core * CB + c_lane - c_group * CB
    cut = one_hot(jnp.logical_and(c_group < GROUPS, c_src == c_want))
    for half in range(2):
        a = half * CAP_ROWS + USED_ROWS
        stage[a : a + CAP_ROWS - USED_ROWS, :] = jnp.zeros((CAP_ROWS - USED_ROWS, LANES), F32)
    stride = 2 * USED_ROWS
    unroll = USED_ROWS // 2

    def block_to(d, n):
        return send(
            outgo.at[d, n], income.at[j], o_send.at[d, n], o_recv.at[j],
            comp=c - core + n, pts=d,
        )

    def owner_of(s):
        return lax.rem(j + 2 * lax.rem(s, NB // 2) + core, NB)

    def pick(d, r, to):
        at = cells.at[pl.ds(d * CELLS + r, (PAIR_GROUPS - 1) * stride + 1)]
        stage[pl.ds(to, 1), :] = merge_rows(tab, at, PAIR_GROUPS, stride, lane, 2 * CB)

    def blocks_of():
        packed = jnp.concatenate([stage[0:CAP_ROWS, :], stage[CAP_ROWS : 2 * CAP_ROWS, :]], axis=1)
        return mm(packed.astype(BF16), cut).astype(BF16)

    def first_rows(q, _):
        for u in range(unroll):
            r = q * unroll + u
            pick(owner_of(1), r, r + (q // 2) * (CAP_ROWS - USED_ROWS))
        return 0

    lax.fori_loop(0, 4, first_rows, 0)

    def owner(s, _):
        before = owner_of(s - 1)
        blocks = blocks_of()
        for r in range(USED_ROWS):
            pick(owner_of(s), r, r)
        for n in range(2):
            outgo[before, n] = blocks[:, n * LANES : (n + 1) * LANES]
            block_to(before, n).start()
        for r in range(USED_ROWS):
            pick(owner_of(s), USED_ROWS + r, CAP_ROWS + r)
        return 0

    lax.fori_loop(2, NB // 2 + 1, owner, 0)
    last = owner_of(NB // 2)
    blocks = blocks_of()
    outgo[last, 1] = blocks[:, LANES:]
    block_to(last, 1).start()

    @pl.when(core == 1)
    def _():
        outgo[last, 0] = blocks[:, :LANES]
        block_to(last, 0).start()

    @pl.when(core == 0)
    def _():
        income[j] = blocks[:, :LANES]

    def sent(s, _):
        d = lax.rem(j + 2 * s + core, NB)
        block_to(d, 1).wait_send()

        @pl.when(d != j)
        def _():
            block_to(d, 0).wait_send()

        return 0

    lax.fori_loop(0, NB // 2, sent, 0)

    def arrive(s, _):
        d = lax.rem(j + s, NB)

        @pl.when(jnp.logical_or(s > 0, core == 1))
        def _():
            send(
                outgo.at[d, 0], income.at[d], o_send.at[d, 0], o_recv.at[d], comp=mate, pts=d
            ).wait_recv()

        return 0

    lax.fori_loop(0, NB, arrive, 0)

    total = NB * CAP_ROWS
    got = income[...].reshape(total, LANES)
    for pair in range(GROUPS // 2):
        both = mm(got, spread_matrix(2 * pair * CB, (2 * pair + 1) * CB, SLOT_GROUPS))
        tab[2 * pair * total : (2 * pair + 1) * total, :] = both[:, :LANES]
        tab[(2 * pair + 1) * total : (2 * pair + 2) * total, :] = both[:, LANES:]
    put_slots.wait()
    slot_unroll = 32

    def slot_rows(q, _):
        for u in range(slot_unroll):
            r = q * slot_unroll + u
            at = slots.at[0, pl.ds(r, (SLOT_GROUPS - 1) * SLOT_ROWS + 1)]
            stage[pl.ds(r, 1), :] = merge_rows(tab, at, SLOT_GROUPS, SLOT_ROWS, lane)
        return 0

    lax.fori_loop(0, SLOT_ROWS // slot_unroll, slot_rows, 0)
    t_row = iota((SLOT_GROUPS * 16, LANES), 0)
    t_lane = iota((SLOT_GROUPS * 16, LANES), 1)
    group = t_row // 16
    comp = t_row - group * 16
    turn = one_hot(jnp.logical_and(comp < CB, t_lane == group * CB + comp))
    turned = lax.dot_general(
        turn, stage[...].astype(BF16), (((1,), (1,)), ((), ())), preferred_element_type=F32
    )
    for g in range(SLOT_GROUPS):
        size = min(SLOT_ROWS, width - g * SLOT_ROWS)
        out_ref[:, g * SLOT_ROWS : g * SLOT_ROWS + size] = turned[16 * g : 16 * g + CB, :size].astype(BF16)

    for copy in copies + shares:
        copy.wait_send()
    for hop in hops:
        hop.wait_send()


def whole(x, mask, coef, cells, counts, back):
    dma = pltpu.SemaphoreType.DMA
    vmem = pl.BlockSpec(memory_space=pltpu.VMEM)
    hbm = pl.BlockSpec(memory_space=pltpu.HBM)
    wrapped = PAD + LON + PAD
    chunk = CHUNK + 32
    return pl.pallas_call(
        whole_kernel,
        out_shape=jax.ShapeDtypeStruct((CB, back.shape[1]), BF16),
        in_specs=[hbm, hbm, vmem, hbm, hbm, hbm],
        out_specs=vmem,
        scratch_shapes=[
            pltpu.VMEM(x.shape, BF16),
            pltpu.VMEM((NB, SEG, 2 * LANES), BF16),
            pltpu.VMEM((NB, SEG, 2 * LANES), BF16),
            pltpu.VMEM((NB, SEG, LANES), BF16),
            pltpu.VMEM((NB, SEG, LANES), BF16),
            pltpu.VMEM((2, 3 * SEG, 2 * LANES), F32),
            pltpu.VMEM((ROWS, LON), jnp.int32),
            pltpu.VMEM((ROWS, LON), jnp.int32),
            pltpu.VMEM((ROWS, LON), jnp.int32),
            pltpu.VMEM((3 * ROWS, LON), F32),
            pltpu.VMEM((wrapped, LANES), F32),
            pltpu.VMEM((LON, LANES), F32),
            pltpu.VMEM((wrapped, LANES), F32),
            pltpu.VMEM((wrapped, LANES), F32),
            pltpu.VMEM((chunk, LANES), F32),
            pltpu.VMEM((chunk, LANES), F32),
            pltpu.VMEM((LON, LANES), BF16),
            pltpu.VMEM((LON, LANES), BF16),
            pltpu.VMEM((ROWS * LON, LANES), F32),
            pltpu.VMEM((SLOT_ROWS, LANES), F32),
            pltpu.VMEM((NB, 2, CAP_ROWS, LANES), BF16),
            pltpu.VMEM((NB, CAP_ROWS, LANES), BF16),
            pltpu.VMEM(back.shape, jnp.int32),
            pltpu.VMEM((1, SLOT_ROWS * SLOT_GROUPS), jnp.int32),
            pltpu.SMEM((NB * CELLS,), jnp.int32),
            pltpu.SMEM((NB, NB), jnp.int32),
            pltpu.SMEM((1, SLOT_ROWS * SLOT_GROUPS), jnp.int32),
            dma((NB,)), dma((NB,)), dma((NB,)), dma((NB,)), dma((2,)), dma((2,)), dma((6,)), dma((NB,)),
            dma((LON // CHUNK,)), dma((LON // CHUNK,)), dma((NB, 2)), dma((NB,)),
        ],
        compiler_params=pltpu.CompilerParams(
            collective_id=0, has_side_effects=True, vmem_limit_bytes=60 << 20
        ),
        name="propagate_and_return",
    )(x, mask, coef, cells, counts, back)


def coefficients(comp_here, pts_here):
    grid_rows = ROWS * NB
    lane = jnp.arange(LANES, dtype=jnp.int32)
    rr = lane // CB
    comp = comp_here * CB + lane % CB
    quad = comp_here % 4
    north = quad < 2
    band_row = jnp.where(north, rr - ITERS, ROWS - 1 + ITERS - rr)
    row = (pts_here * ROWS + band_row).astype(F32)

    def cosines(row_ids):
        radians = (45.0 + 0.1 * (row_ids + 0.5 - 0.5 * grid_rows)) * (math.pi / 180.0)
        return jnp.cos(radians), jnp.cos(radians + 0.05 * math.pi / 180.0)

    cos_mid, cos_upper = cosines(row)
    cos_lower = cosines(row - 1.0)[1]
    freq = (comp // ND).astype(F32)
    angle = ((comp % ND).astype(F32) + 0.5) * (2.0 * math.pi / ND)
    top = math.cos((45.0 + 0.05 * grid_rows) * math.pi / 180.0)
    speed = 0.6 * top * jnp.power(jnp.float32(1.1), -freq)
    east_x = jnp.abs(speed * jnp.cos(angle))
    north_y = jnp.abs(speed * jnp.sin(angle))
    ax = east_x / cos_mid
    up = north_y * jnp.where(north, cos_lower, cos_upper) / cos_mid
    dn = north_y * jnp.where(north, cos_upper, cos_lower) / cos_mid
    live = rr < ROWS + ITERS
    rows = [jnp.where(live, value, 0.0) for value in (ax, up, dn)]
    return jnp.stack(rows + [jnp.zeros((LANES,), F32)] * 5)


def local(spectra, land_mask, send_rows, row_counts, return_index):
    comp_here = lax.axis_index("comp")
    pts_here = lax.axis_index("pts")
    coef = coefficients(comp_here, pts_here)
    return whole(spectra, land_mask, coef, send_rows, row_counts, return_index)


def solution(mesh):
    placed = (P("comp", "pts"), P("pts", None), P("pts", None, None), P(), P("pts", None))
    return jax.shard_map(
        local, mesh=mesh, in_specs=placed, out_specs=P("comp", "pts"), check_vma=False
    )
```
